256 devices in a mesh: layer: 4 (over x_lo, core), tile: 64 (over x_hi, y, z).
Axes of the slice: x: 4 (x_hi: 2, x_lo: 2; x = x_hi * 2 + x_lo), y: 4, z: 8, core: 2. Of those that a mesh axis runs over, the one named last changes fastest.
Arguments:
- screens: bfloat16 [12, 8192, 10240], P('layer', 'tile'), may hold values from -5 to 5
- chosen: int32 [8], P('layer'), may hold values from 0 to 2
- row_shift: int32 [8], P('layer'), may hold values from 0 to 127, as said below
- column_shift: int32 [8], P('layer'), may hold values from 0 to 1920, as said below
- fractions: float32 [8, 2], P('layer'), may hold values from 0 to 1
- pistons: float32 [798], replicated, may hold values from -3 to 3
- segment_map: int32 [32, 32], replicated, may hold values from 0 to 797
- amplitude: bfloat16 [8192, 8192], P('tile'), may hold values from 0 to 10
Outputs:
- intensity: float32 [8192, 8192], P('tile', 'layer')
The draws below stay inside these ranges and needn't reach their ends.
Inputs may be any that keep to these rules, and one draw needn't show every extreme that they name: Entry s takes one of its own group's screens: stored screen (s // 2) * 3 + chosen[s]. `row_shift`: both ends of the range are taken in every draw. `column_shift`: both ends of the range are taken in every draw.
All inputs are finite; a program needn't handle non-finite values.
Results may differ from the reference program's by a relative error of at most 0.0003.
Values may be sent and summed in bfloat16 or wider, within the bound.
A program may use at most 128 MiB of HBM per device.

```python
import math
import jax
import jax.numpy as jnp
from jax import lax

PUPIL = 8192
PADDED = 16384
SCREEN = 10240
GROUP_LAYERS = 3
PICKED = 2
SEGMENTS = 798
SEG_GRID = 32
DOT_RADIUS = 2
ROWS_DEV = 128
STORED = 12
PICKED_ALL = 8


def shifts_within(key, count, bound):
    first, second = jax.random.split(key)
    values = jax.random.randint(first, (count,), 0, bound + 1, jnp.int32)
    order = jax.random.permutation(second, count)
    return values.at[order[0]].set(bound).at[order[1]].set(0)


def draw_row_shift(key, part):
    return shifts_within(jax.random.fold_in(key, 11), PICKED_ALL, ROWS_DEV - 1)


def draw_column_shift(key, part):
    return shifts_within(jax.random.fold_in(key, 23), PICKED_ALL, SCREEN - PUPIL - 128)


def draw_screens(key, part):
    keys = jax.random.split(jax.random.fold_in(key, 51), 5)
    shape = (STORED, PUPIL, SCREEN)
    speckle = jnp.clip(jax.random.normal(keys[0], shape, jnp.float32) * 0.6, -3.0, 3.0)
    height = jax.random.uniform(keys[1], (STORED, 1, 1), jnp.float32, 0.5, 1.0)
    period = jnp.exp(jax.random.uniform(keys[2], (STORED, 1, 1), jnp.float32, math.log(PUPIL / 4.0), math.log(float(PUPIL))))
    heading = jax.random.uniform(keys[3], (STORED, 1, 1), jnp.float32, 0.0, 2.0 * math.pi)
    offset = jax.random.uniform(keys[4], (STORED, 1, 1), jnp.float32, 0.0, 2.0 * math.pi)
    row_place = jnp.arange(PUPIL, dtype=jnp.float32)[None, :, None]
    column_place = jnp.arange(SCREEN, dtype=jnp.float32)[None, None, :]
    argument = 2.0 * math.pi / period * (jnp.cos(heading) * row_place + jnp.sin(heading) * column_place) + offset
    smooth = height * jnp.sin(argument)
    return jnp.clip(speckle + smooth, -5.0, 5.0).astype(jnp.bfloat16)


def draw_amplitude(key, part):
    first, second, third = jax.random.split(jax.random.fold_in(key, 37), 3)
    reach = 0.5 * math.log(10.0)
    base = jnp.exp(jax.random.uniform(first, (PUPIL, PUPIL), jnp.float32, math.log(0.1), 0.0))
    row_scale = jnp.exp(jax.random.uniform(second, (PUPIL, 1), jnp.float32, -reach, reach))
    column_scale = jnp.exp(jax.random.uniform(third, (1, PUPIL), jnp.float32, -reach, reach))
    return (base * row_scale * column_scale).astype(jnp.bfloat16)


def with_ends(entries, stream_key, low, largest):
    shape = entries.shape
    index_at = [jax.random.randint(jax.random.fold_in(stream_key, axis), (), 0, shape[axis]) for axis in range(len(shape))]
    entries = entries.at[tuple(index_at)].set(low)
    longest = shape.index(max(shape))
    index_at[longest] = (index_at[longest] + 1) % shape[longest]
    return entries.at[tuple(index_at)].set(largest)


def level_of(own_key, shape, cuts, smallest, top_value):
    def one(position, blocks):
        draws = jax.random.uniform(jax.random.fold_in(jax.random.fold_in(own_key, 6), position), (blocks,), jnp.float32, smallest / len(cuts), top_value / len(cuts))
        return jnp.repeat(jnp.exp(draws), shape[position] // blocks).reshape((-1,) + (1,) * (len(shape) - position - 1))

    loudness = one(*cuts[0])
    for cut in cuts[1:]:
        loudness = loudness * one(*cut)
    return loudness


def centred(stream_key, extent, scale, most, held_as=jnp.bfloat16):
    array = jax.random.normal(stream_key, extent, jnp.float32) * scale
    return jnp.minimum(jnp.maximum(array, -most), most).astype(held_as)


def setup_inputs(seed: int = 0) -> dict:
    splits = jax.random.split(jax.random.key(seed), 9)
    screens = draw_screens(jax.random.fold_in(splits[8], 71), 0)
    chosen = with_ends(jax.random.randint(splits[1], (PICKED_ALL,), 0, GROUP_LAYERS), jax.random.fold_in(splits[1], 1), 0, GROUP_LAYERS - 1).astype(jnp.int32)
    row_shift = draw_row_shift(jax.random.fold_in(splits[8], 71), 0)
    column_shift = draw_column_shift(jax.random.fold_in(splits[8], 71), 0)
    fractions = jnp.clip(1.0 * jax.random.uniform(splits[4], (PICKED_ALL, 2), jnp.float32) ** level_of(splits[4], (PICKED_ALL, 2), ((0, 4),), -0.2, 0.2), 0.0, 1.0)
    pistons = centred(splits[5], (SEGMENTS,), 0.5, 3.0, jnp.float32)
    segment_map = with_ends(jax.random.randint(splits[6], (SEG_GRID, SEG_GRID), 0, SEGMENTS), jax.random.fold_in(splits[6], 1), 0, SEGMENTS - 1).astype(jnp.int32)
    amplitude = draw_amplitude(jax.random.fold_in(splits[8], 71), 0)
    return dict(screens=screens, chosen=chosen, row_shift=row_shift, column_shift=column_shift, fractions=fractions, pistons=pistons, segment_map=segment_map, amplitude=amplitude)


phase_step = math.pi / 2
highest = lax.Precision.HIGHEST


def layer_phase(screen, rows_ahead, columns_ahead, frac_row, frac_column):
    wide = lax.dynamic_slice_in_dim(screen, columns_ahead, PUPIL + 1, 1).astype(jnp.float32)
    across = (1.0 - frac_column) * wide[:, :PUPIL] + frac_column * wide[:, 1:]
    rolled = jnp.roll(across, -rows_ahead, axis=0)
    return (1.0 - frac_row) * rolled + frac_row * jnp.roll(rolled, -1, axis=0)


def dot_table(positions):
    frequency = jnp.arange(2 * DOT_RADIUS + 1, dtype=jnp.int32) - DOT_RADIUS
    steps = (frequency[:, None] * positions[None, :]) % PADDED
    angle = (-2.0 * math.pi / PADDED) * steps.astype(jnp.float32)
    return jnp.cos(angle), jnp.sin(angle)


def complex_einsum(form, first_pair, second_pair):
    real = jnp.einsum(form, first_pair[0], second_pair[0], precision=highest) - jnp.einsum(form, first_pair[1], second_pair[1], precision=highest)
    imaginary = jnp.einsum(form, first_pair[0], second_pair[1], precision=highest) + jnp.einsum(form, first_pair[1], second_pair[0], precision=highest)
    return real, imaginary


def reference(screens, chosen, row_shift, column_shift, fractions, pistons, segment_map, amplitude):
    phase = jnp.zeros((PUPIL, PUPIL), jnp.float32)
    for entry in range(PICKED_ALL):
        group = entry // PICKED
        which = (group * GROUP_LAYERS + chosen[entry]).astype(jnp.int32)
        screen = lax.dynamic_index_in_dim(screens, which, 0, keepdims=False)
        phase = phase + layer_phase(screen, row_shift[entry], column_shift[entry], fractions[entry, 0], fractions[entry, 1])
    grid = jnp.take(pistons, segment_map)
    block = PUPIL // SEG_GRID
    phase = phase + jnp.repeat(jnp.repeat(grid, block, axis=0), block, axis=1)
    magnitude = amplitude.astype(jnp.float32)
    field = (magnitude * jnp.cos(phase), magnitude * jnp.sin(phase))
    table = dot_table(jnp.arange(PUPIL, dtype=jnp.int32))
    half = complex_einsum("fc,rc->fr", table, field)
    coefficient = complex_einsum("gr,fr->gf", table, half)
    frequency = jnp.arange(2 * DOT_RADIUS + 1, dtype=jnp.int32) - DOT_RADIUS
    inside = ((frequency[:, None] ** 2 + frequency[None, :] ** 2) <= DOT_RADIUS ** 2).astype(jnp.float32) / (PADDED * PADDED)
    turn_real = (math.cos(phase_step) - 1.0) * inside
    turn_imaginary = math.sin(phase_step) * inside
    weights = (coefficient[0] * turn_real - coefficient[1] * turn_imaginary, coefficient[0] * turn_imaginary + coefficient[1] * turn_real)
    conjugate = (table[0], -table[1])
    wave = complex_einsum("gf,fc->gc", weights, conjugate)
    wave = complex_einsum("gr,gc->rc", conjugate, wave)
    real = field[0] + wave[0]
    imaginary = field[1] + wave[1]
    return real * real + imaginary * imaginary
```

```python
import functools
import math

import jax
import jax.numpy as jnp
from jax import lax
from jax.experimental import pallas as pl
from jax.experimental.pallas import tpu as pltpu
from jax.sharding import PartitionSpec as P

PUPIL = 8192
PADDED = 16384
SEG_GRID = 32
DOT_RADIUS = 2
ROWS = 128
SHARE = 2048
CHUNK = 256
CHUNKS = SHARE // CHUNK
WIDE = SHARE + 128
PIECES = 3
LINK = jnp.float32
phase_step = math.pi / 2
f32 = jnp.float32
bf16 = jnp.bfloat16
MESH = pl.DeviceIdType.MESH


def nearest(x):
    return jnp.floor(x + 0.5)


def turn_sincos(u):
    r = u - nearest(u)
    q = nearest(4.0 * r)
    x = (r - 0.25 * q) * (2.0 * math.pi)
    z = x * x
    s = x * (1.0 + z * (-1.0 / 6 + z * (1.0 / 120 + z * (-1.0 / 5040 + z * (1.0 / 362880)))))
    c = 1.0 + z * (-0.5 + z * (1.0 / 24 + z * (-1.0 / 720 + z * (1.0 / 40320))))
    odd = jnp.abs(q) == 1.0
    cos = jnp.where(odd, s, c)
    sin = jnp.where(odd, c, s)
    cos = jnp.where((q == 1.0) | (jnp.abs(q) == 2.0), -cos, cos)
    sin = jnp.where((q == -1.0) | (jnp.abs(q) == 2.0), -sin, sin)
    return cos, sin


def to_link(u):
    return u


def from_link(v):
    return v


def place_kernel(
    screens, chosen, row_shift, column_shift, fractions, pistons, segment_map,
    aligned, prm, steps, raw, ready, load_sem, store_sem,
):
    layer = lax.axis_index("layer")
    tile = lax.axis_index("tile")
    sibling = (layer // 2) * 2 + 1 - layer % 2
    order = ((sibling + 2) % 4, (layer + 2) % 4, sibling, layer)

    def load(area, e):
        start = (column_shift[e] // 128 + 16 * area) * 128
        return pltpu.make_async_copy(
            screens.at[chosen[e], :, pl.ds(pl.multiple_of(start, 128), WIDE)],
            raw.at[area, e],
            load_sem.at[area, e],
        )

    def store(area):
        return pltpu.make_async_copy(ready.at[area], aligned.at[area], store_sem.at[area])

    for area in order:
        for e in range(2):
            load(area, e).start()
    for e in range(2):
        prm[pl.ds(4 * e, 1), :] = jnp.full((1, 128), row_shift[e], jnp.int32).astype(f32)
        prm[pl.ds(4 * e + 1, 1), :] = jnp.full((1, 128), fractions[e, 0], f32)
        prm[pl.ds(4 * e + 2, 1), :] = jnp.full((1, 128), fractions[e, 1], f32)
        prm[pl.ds(4 * e + 3, 1), :] = jnp.zeros((1, 128), f32)
    for k in range(CHUNKS):
        piston = pistons[segment_map[tile // 2, layer * CHUNKS + k]]
        steps[pl.ds(k, 1), :] = jnp.full((1, 128), piston * (0.5 / math.pi), f32)
    lane = lax.broadcasted_iota(jnp.int32, (ROWS, 128), 1)
    for area in order:
        for e in range(2):
            load(area, e).wait()
            part = column_shift[e] % 128
            keep = lane < 128 - part

            def rolled(j):
                block = raw[area, e, :, pl.ds(128 * j, 128)].astype(f32)
                return pltpu.roll(block, (128 - part) % 128, 1)

            previous = rolled(0)
            for j in range(16):
                following = rolled(j + 1)
                ready[area, e, :, pl.ds(128 * j, 128)] = jnp.where(
                    keep, previous, following
                ).astype(bf16)
                previous = following
            ready[area, e, :, pl.ds(SHARE, 128)] = previous.astype(bf16)
        store(area).start()
    for area in order:
        store(area).wait()


def kernel(
    placed, prm, steps, amplitude, out,
    amp, aligned, shared, sib_prm, taps, weights, product, own,
    x_out, x_in, z_out, z_in, field_re, field_im, rows_t, cols_t, acc, message, first, second,
    load_sem, share_send, share_recv, prm_sem, x_send, x_recv, z_send, z_recv, one_sem, two_sem,
):
    layer = lax.axis_index("layer")
    tile = lax.axis_index("tile")
    pair, core = layer // 2, layer % 2
    sibling = pair * 2 + 1 - core
    partner = (1 - pair) * 2 + core
    crossed = (1 - pair) * 2 + 1 - core
    before = (tile + 63) % 64
    after = (tile + 1) % 64

    depth = tile % 8
    slab = tile // 8

    def near_peer(d):
        place = (depth * 2 + core + d) % 16
        return pair * 2 + place % 2, slab * 8 + place // 2

    def far_peer(d):
        place = (slab * 2 + pair + d) % 16
        return (place % 2) * 2 + core, (place // 2) * 8 + depth

    loads = [
        pltpu.make_async_copy(placed.at[area], aligned.at[slot], load_sem.at[slot])
        for slot, area in enumerate((partner, layer))
    ]
    loads.append(
        pltpu.make_async_copy(
            amplitude.at[:, pl.ds(pl.multiple_of(layer * SHARE, SHARE), SHARE)],
            amp,
            load_sem.at[2],
        )
    )
    for load in loads:
        load.start()

    barrier = pltpu.get_barrier_semaphore()
    for d in range(1, 16):
        pl.semaphore_signal(barrier, inc=1, device_id=near_peer(d), device_id_type=MESH)
        pl.semaphore_signal(barrier, inc=1, device_id=far_peer(d), device_id_type=MESH)
    pl.semaphore_signal(barrier, inc=1, device_id=(layer, before), device_id_type=MESH)
    pl.semaphore_signal(barrier, inc=1, device_id=(layer, after), device_id_type=MESH)

    row_id = lax.broadcasted_iota(jnp.int32, (ROWS, 128), 0) + tile * ROWS
    for k in (1, 2):
        cos, sin = turn_sincos((row_id * k).astype(f32) * (1.0 / PADDED))
        for half in range(2):
            rows_t[2 * k - 2, :, pl.ds(128 * half, 128)] = cos
            rows_t[2 * k - 1, :, pl.ds(128 * half, 128)] = sin
    kind = lax.broadcasted_iota(jnp.int32, (8, SHARE), 0)
    col_id = lax.broadcasted_iota(jnp.int32, (8, SHARE), 1) + layer * SHARE
    cos, sin = turn_sincos((col_id * ((kind + 1) // 2)).astype(f32) * (1.0 / PADDED))
    table = jnp.where((kind == 2) | (kind == 4), sin, cos)
    cols_t[...] = jnp.where(kind < 5, table, 0.0)
    acc[...] = jnp.zeros_like(acc)

    pl.semaphore_wait(barrier, 32)
    send_prm = pltpu.make_async_remote_copy(
        src_ref=prm, dst_ref=sib_prm, send_sem=prm_sem.at[0], recv_sem=prm_sem.at[1],
        device_id=(sibling, tile), device_id_type=MESH,
    )
    send_prm.start()
    def share(area, slot):
        return pltpu.make_async_remote_copy(
            src_ref=placed.at[area], dst_ref=shared.at[slot],
            send_sem=share_send.at[slot], recv_sem=share_recv.at[slot],
            device_id=(sibling, tile), device_id_type=MESH,
        )

    share_far = share(crossed, 0)
    share_far.start()
    share_near = share(sibling, 1)
    share_near.start()

    send_prm.wait()
    gap = (
        lax.broadcasted_iota(jnp.int32, (256, 128), 1)
        - lax.broadcasted_iota(jnp.int32, (256, 128), 0)
        + 128
    ).astype(f32)
    for source in range(2):
        table = prm if source == 0 else sib_prm
        for e in range(2):
            shift = table[pl.ds(4 * e, 1), :]
            frac_row = table[pl.ds(4 * e + 1, 1), :]
            frac_col = table[pl.ds(4 * e + 2, 1), :]
            down = jnp.where(gap == shift, 1.0 - frac_row, 0.0) + jnp.where(
                gap == shift + 1.0, frac_row, 0.0
            )
            for tap in range(2):
                left = down * ((frac_col if tap else 1.0 - frac_col) * (0.5 / math.pi))
                place = (source * 2 + e) * 256 + tap * 128
                for piece in range(PIECES):
                    part = left.astype(bf16)
                    weights[pl.ds(256 * piece, 256), pl.ds(place, 128)] = part
                    left = left - part.astype(f32)

    def fill(slot, k):
        for source in range(2):
            for e in range(2):
                cols = pl.ds(pl.multiple_of(k * CHUNK, CHUNK), CHUNK + 128)
                block = aligned[slot, e, :, cols] if source == 0 else shared[slot, e, :, cols]
                place = (source * 2 + e) * 256
                taps[pl.ds(place, 128), :] = block[:, :CHUNK]
                moved = pltpu.roll(block.astype(f32), CHUNK + 127, 1)
                taps[pl.ds(place + 128, 128), :] = moved[:, :CHUNK].astype(bf16)
        product[...] = jnp.dot(weights[...], taps[...], preferred_element_type=f32)

    def summed(first_row, rows):
        total = product[pl.ds(first_row, rows), :]
        for piece in range(1, PIECES):
            total = total + product[pl.ds(256 * piece + first_row, rows), :]
        return total

    def across(half, k):
        return pltpu.make_async_remote_copy(
            src_ref=x_out.at[half, k], dst_ref=x_in.at[half, k],
            send_sem=x_send.at[half, k], recv_sem=x_recv.at[half, k],
            device_id=(partner, tile), device_id_type=MESH,
        )

    def upward(k):
        return pltpu.make_async_remote_copy(
            src_ref=z_out.at[k], dst_ref=z_in.at[k],
            send_sem=z_send.at[k], recv_sem=z_recv.at[k],
            device_id=(layer, before), device_id_type=MESH,
        )

    loads[0].wait()
    share_far.wait()

    @pl.loop(0, CHUNKS)
    def _(k):
        fill(0, k)
        for block in range(8):
            x_out[block // 4, k, pl.ds(32 * (block % 4), 32), :] = to_link(
                summed(32 * block, 32)
            )
        across(0, k).start()

    @pl.loop(0, CHUNKS)
    def _(k):
        across(1, k).start()

    loads[1].wait()
    share_near.wait()

    @pl.loop(0, CHUNKS)
    def _(k):
        fill(1, k)
        for block in range(8):
            own[block // 4, k, pl.ds(32 * (block % 4), 32), :] = summed(32 * block, 32)

    @pl.loop(0, CHUNKS)
    def _(k):
        across(0, k).wait()
        for block in range(4):
            rows = pl.ds(32 * block, 32)
            z_out[k, rows, :] = to_link(own[0, k, rows, :] + from_link(x_in[0, k, rows, :]))
        upward(k).start()

    loads[2].wait()

    @pl.loop(0, CHUNKS)
    def _(k):
        across(1, k).wait()
        upward(k).wait()
        line = steps[pl.ds(k, 1), :]
        piston = jnp.concatenate([line, line], axis=1)
        sums = [jnp.zeros((8, CHUNK), f32) for _ in range(10)]
        cols = pl.ds(pl.multiple_of(k * CHUNK, CHUNK), CHUNK)
        for block in range(8):
            rows = pl.ds(16 * block, 16)
            turns = (
                own[1, k, rows, :]
                + from_link(x_in[1, k, rows, :])
                + from_link(z_in[k, rows, :])
                + piston
            )
            cos, sin = turn_sincos(turns)
            size = amp[rows, cols].astype(f32)
            real, imag = size * cos, size * sin
            field_re[k, rows, :] = real
            field_im[k, rows, :] = imag
            for base, part in ((0, real), (5, imag)):
                sums[base] = sums[base] + (part[:8] + part[8:])
                for j in range(4):
                    wide = part * rows_t[j, rows, :]
                    sums[base + 1 + j] = sums[base + 1 + j] + (wide[:8] + wide[8:])
        for j in range(10):
            line = jnp.sum(sums[j], axis=0, keepdims=True)
            spread = line * cols_t[:, cols]
            acc[j] = acc[j] + (spread[:, :128] + spread[:, 128:])

    spot = lax.broadcasted_iota(jnp.int32, (8, 128), 1)
    packed = jnp.zeros((8, 128), f32)
    for j in range(10):
        packed = jnp.where(spot == j, jnp.sum(acc[j], axis=1, keepdims=True), packed)
    message[0] = packed

    def exchange(slot, peer, target, sem):
        copies = [
            pltpu.make_async_remote_copy(
                src_ref=message.at[slot], dst_ref=target.at[d],
                send_sem=sem.at[0, d], recv_sem=sem.at[1, d],
                device_id=peer(d), device_id_type=MESH,
            )
            for d in range(1, 16)
        ]
        for copy in copies:
            copy.start()
        total = message[slot]
        for copy in copies:
            copy.wait()
        for d in range(1, 16):
            total = total + target[d]
        return total

    message[1] = exchange(0, near_peer, first, one_sem)
    total = exchange(1, far_peer, second, two_sem)

    row_kind = spot % 5
    col_kind = lax.broadcasted_iota(jnp.int32, (8, 128), 0)
    row_freq = (row_kind + 1) // 2
    col_freq = (col_kind + 1) // 2
    inside = (row_freq * row_freq + col_freq * col_freq <= DOT_RADIUS**2) & (spot < 10)
    factor = (
        jnp.where(inside, 1.0 / (PADDED * PADDED), 0.0)
        * jnp.where(row_kind > 0, 2.0, 1.0)
        * jnp.where(col_kind > 0, 2.0, 1.0)
    )
    turned = jnp.where(spot < 5, -pltpu.roll(total, 123, 1), pltpu.roll(total, 5, 1))
    mix = factor * ((math.cos(phase_step) - 1.0) * total + math.sin(phase_step) * turned)
    for k in range(CHUNKS):
        cols = pl.ds(CHUNK * k, CHUNK)
        lines = [
            jnp.sum(mix[:, j : j + 1] * cols_t[:, cols], axis=0, keepdims=True) for j in range(10)
        ]
        for block in range(8):
            rows = pl.ds(16 * block, 16)
            real = field_re[k, rows, :] + lines[0]
            imag = field_im[k, rows, :] + lines[5]
            for j in range(4):
                table = rows_t[j, rows, :]
                real = real + table * lines[1 + j]
                imag = imag + table * lines[6 + j]
            out[rows, cols] = real * real + imag * imag


def body(screens, chosen, row_shift, column_shift, fractions, pistons, segment_map, amplitude):
    hbm = pl.BlockSpec(memory_space=pl.ANY)
    smem = pl.BlockSpec(memory_space=pltpu.SMEM)
    vmem = pl.BlockSpec(memory_space=pltpu.VMEM)
    dma = pltpu.SemaphoreType.DMA
    placed, prm, steps = pl.pallas_call(
        place_kernel,
        out_shape=(
            jax.ShapeDtypeStruct((4, 2, ROWS, WIDE), bf16),
            jax.ShapeDtypeStruct((8, 128), f32),
            jax.ShapeDtypeStruct((8, 128), f32),
        ),
        in_specs=[hbm, smem, smem, smem, smem, smem, smem],
        out_specs=(hbm, vmem, vmem),
        scratch_shapes=[
            pltpu.VMEM((4, 2, ROWS, WIDE), bf16),
            pltpu.VMEM((4, 2, ROWS, WIDE), bf16),
            dma((4, 2)),
            dma((4,)),
        ],
        compiler_params=pltpu.CompilerParams(vmem_limit_bytes=32 * 1024 * 1024),
    )(screens, chosen, row_shift, column_shift, fractions, pistons, segment_map)
    return pl.pallas_call(
        kernel,
        out_shape=jax.ShapeDtypeStruct((ROWS, SHARE), f32),
        in_specs=[hbm, vmem, vmem, hbm],
        out_specs=vmem,
        scratch_shapes=[
            pltpu.VMEM((ROWS, SHARE), bf16),
            pltpu.VMEM((2, 2, ROWS, WIDE), bf16),
            pltpu.VMEM((2, 2, ROWS, WIDE), bf16),
            pltpu.VMEM((8, 128), f32),
            pltpu.VMEM((1024, CHUNK), bf16),
            pltpu.VMEM((256 * PIECES, 1024), bf16),
            pltpu.VMEM((256 * PIECES, CHUNK), f32),
            pltpu.VMEM((2, CHUNKS, ROWS, CHUNK), f32),
            pltpu.VMEM((2, CHUNKS, ROWS, CHUNK), LINK),
            pltpu.VMEM((2, CHUNKS, ROWS, CHUNK), LINK),
            pltpu.VMEM((CHUNKS, ROWS, CHUNK), LINK),
            pltpu.VMEM((CHUNKS, ROWS, CHUNK), LINK),
            pltpu.VMEM((CHUNKS, ROWS, CHUNK), f32),
            pltpu.VMEM((CHUNKS, ROWS, CHUNK), f32),
            pltpu.VMEM((4, ROWS, CHUNK), f32),
            pltpu.VMEM((8, SHARE), f32),
            pltpu.VMEM((10, 8, 128), f32),
            pltpu.VMEM((2, 8, 128), f32),
            pltpu.VMEM((16, 8, 128), f32),
            pltpu.VMEM((16, 8, 128), f32),
            dma((3,)),
            dma((2,)),
            dma((2,)),
            dma((2,)),
            dma((2, CHUNKS)),
            dma((2, CHUNKS)),
            dma((CHUNKS,)),
            dma((CHUNKS,)),
            dma((2, 16)),
            dma((2, 16)),
        ],
        compiler_params=pltpu.CompilerParams(
            collective_id=0, has_side_effects=True, vmem_limit_bytes=48 * 1024 * 1024
        ),
    )(placed, prm, steps, amplitude)


def solution(mesh):
    return jax.shard_map(
        body,
        mesh=mesh,
        in_specs=(
            P("layer", "tile", None),
            P("layer"),
            P("layer"),
            P("layer"),
            P("layer", None),
            P(),
            P(),
            P("tile", None),
        ),
        out_specs=P("tile", "layer"),
        check_vma=False,
    )
```

```python
import functools
import math

import jax
import jax.numpy as jnp
from jax import lax
from jax.experimental import pallas as pl
from jax.experimental.pallas import tpu as pltpu
from jax.sharding import PartitionSpec as P

PUPIL = 8192
PADDED = 16384
SEG_GRID = 32
DOT_RADIUS = 2
ROWS = 128
SHARE = 2048
CHUNK = 256
CHUNKS = SHARE // CHUNK
WIDE = SHARE + 128
PIECES = 3
LINK = jnp.bfloat16
SPAN = 500.0
phase_step = math.pi / 2
f32 = jnp.float32
bf16 = jnp.bfloat16
MESH = pl.DeviceIdType.MESH


def nearest(x):
    return jnp.floor(x + 0.5)


def turn_sincos(u):
    r = u - nearest(u)
    q = nearest(4.0 * r)
    x = (r - 0.25 * q) * (2.0 * math.pi)
    z = x * x
    s = x * (1.0 + z * (-1.0 / 6 + z * (1.0 / 120 + z * (-1.0 / 5040 + z * (1.0 / 362880)))))
    c = 1.0 + z * (-0.5 + z * (1.0 / 24 + z * (-1.0 / 720 + z * (1.0 / 40320))))
    odd = jnp.abs(q) == 1.0
    cos = jnp.where(odd, s, c)
    sin = jnp.where(odd, c, s)
    cos = jnp.where((q == 1.0) | (jnp.abs(q) == 2.0), -cos, cos)
    sin = jnp.where((q == -1.0) | (jnp.abs(q) == 2.0), -sin, sin)
    return cos, sin


def to_link(u):
    r = u - nearest(u)
    v = jnp.exp2(jnp.abs(r) * SPAN - 0.25 * SPAN)
    return jnp.where(r < 0.0, -v, v).astype(LINK)


def from_link(v):
    v = v.astype(f32)
    r = jnp.log(jnp.abs(v)) * (1.0 / (math.log(2.0) * SPAN)) + 0.25
    return jnp.where(v < 0.0, -r, r)


def place_kernel(
    screens, chosen_hbm, row_shift_hbm, column_shift_hbm, fractions_hbm, pistons_hbm, map_hbm,
    aligned, prm, steps,
    chosen, column_shift, row_shift, fractions, pistons, segment_map,
    raw, ready, small_sem, load_sem, store_sem,
):
    small = [
        pltpu.make_async_copy(source, target, small_sem.at[i])
        for i, (source, target) in enumerate(
            (
                (chosen_hbm, chosen),
                (column_shift_hbm, column_shift),
                (row_shift_hbm, row_shift),
                (fractions_hbm, fractions),
                (pistons_hbm, pistons),
                (map_hbm, segment_map),
            )
        )
    ]
    for copy in small:
        copy.start()
    layer = lax.axis_index("layer")
    tile = lax.axis_index("tile")
    sibling = (layer // 2) * 2 + 1 - layer % 2
    order = ((sibling + 2) % 4, (layer + 2) % 4, sibling, layer)

    def load(area, e):
        start = (column_shift[e] // 128 + 16 * area) * 128
        return pltpu.make_async_copy(
            screens.at[chosen[e], :, pl.ds(pl.multiple_of(start, 128), WIDE)],
            raw.at[area, e],
            load_sem.at[area, e],
        )

    def store(area):
        return pltpu.make_async_copy(ready.at[area], aligned.at[area], store_sem.at[area])

    for copy in small[:2]:
        copy.wait()
    for area in order:
        for e in range(2):
            load(area, e).start()
    for copy in small[2:]:
        copy.wait()
    for e in range(2):
        prm[pl.ds(4 * e, 1), :] = jnp.full((1, 128), row_shift[e], jnp.int32).astype(f32)
        prm[pl.ds(4 * e + 1, 1), :] = jnp.full((1, 128), fractions[e, 0], f32)
        prm[pl.ds(4 * e + 2, 1), :] = jnp.full((1, 128), fractions[e, 1], f32)
        prm[pl.ds(4 * e + 3, 1), :] = jnp.zeros((1, 128), f32)
    for k in range(CHUNKS):
        piston = pistons[segment_map[tile // 2, layer * CHUNKS + k]]
        steps[pl.ds(k, 1), :] = jnp.full((1, 128), piston * (0.5 / math.pi), f32)
    lane = lax.broadcasted_iota(jnp.int32, (ROWS, 128), 1)
    for area in order:
        for e in range(2):
            load(area, e).wait()
            part = column_shift[e] % 128
            keep = lane < 128 - part

            def rolled(j):
                block = raw[area, e, :, pl.ds(128 * j, 128)].astype(f32)
                return pltpu.roll(block, (128 - part) % 128, 1)

            previous = rolled(0)
            for j in range(16):
                following = rolled(j + 1)
                ready[area, e, :, pl.ds(128 * j, 128)] = jnp.where(
                    keep, previous, following
                ).astype(bf16)
                previous = following
            ready[area, e, :, pl.ds(SHARE, 128)] = previous.astype(bf16)
        store(area).start()
    for area in order:
        store(area).wait()


def kernel(
    placed, prm, steps, amplitude, out,
    amp, aligned, shared, sib_prm, taps, weights, product, own,
    x_out, x_in, z_out, z_in, field_re, field_im, rows_t, cols_t, acc, message, first, second,
    load_sem, share_send, share_recv, prm_sem, x_send, x_recv, z_send, z_recv, one_sem, two_sem,
):
    layer = lax.axis_index("layer")
    tile = lax.axis_index("tile")
    pair, core = layer // 2, layer % 2
    sibling = pair * 2 + 1 - core
    partner = (1 - pair) * 2 + core
    crossed = (1 - pair) * 2 + 1 - core
    before = (tile + 63) % 64
    after = (tile + 1) % 64

    depth = tile % 8
    slab = tile // 8

    def near_peer(d):
        place = (depth * 2 + core + d) % 16
        return pair * 2 + place % 2, slab * 8 + place // 2

    def far_peer(d):
        place = (slab * 2 + pair + d) % 16
        return (place % 2) * 2 + core, (place // 2) * 8 + depth

    loads = [
        pltpu.make_async_copy(placed.at[area], aligned.at[slot], load_sem.at[slot])
        for slot, area in enumerate((partner, layer))
    ]
    loads.append(
        pltpu.make_async_copy(
            amplitude.at[:, pl.ds(pl.multiple_of(layer * SHARE, SHARE), SHARE)],
            amp,
            load_sem.at[2],
        )
    )
    for load in loads:
        load.start()

    barrier = pltpu.get_barrier_semaphore()
    for d in range(1, 16):
        pl.semaphore_signal(barrier, inc=1, device_id=near_peer(d), device_id_type=MESH)
        pl.semaphore_signal(barrier, inc=1, device_id=far_peer(d), device_id_type=MESH)
    pl.semaphore_signal(barrier, inc=1, device_id=(layer, before), device_id_type=MESH)
    pl.semaphore_signal(barrier, inc=1, device_id=(layer, after), device_id_type=MESH)

    row_id = lax.broadcasted_iota(jnp.int32, (ROWS, 128), 0) + tile * ROWS
    for k in (1, 2):
        cos, sin = turn_sincos((row_id * k).astype(f32) * (1.0 / PADDED))
        for half in range(2):
            rows_t[2 * k - 2, :, pl.ds(128 * half, 128)] = cos
            rows_t[2 * k - 1, :, pl.ds(128 * half, 128)] = sin
    kind = lax.broadcasted_iota(jnp.int32, (8, SHARE), 0)
    col_id = lax.broadcasted_iota(jnp.int32, (8, SHARE), 1) + layer * SHARE
    cos, sin = turn_sincos((col_id * ((kind + 1) // 2)).astype(f32) * (1.0 / PADDED))
    table = jnp.where((kind == 2) | (kind == 4), sin, cos)
    cols_t[...] = jnp.where(kind < 5, table, 0.0)
    acc[...] = jnp.zeros_like(acc)

    pl.semaphore_wait(barrier, 32)
    send_prm = pltpu.make_async_remote_copy(
        src_ref=prm, dst_ref=sib_prm, send_sem=prm_sem.at[0], recv_sem=prm_sem.at[1],
        device_id=(sibling, tile), device_id_type=MESH,
    )
    send_prm.start()
    def share(area, slot):
        return pltpu.make_async_remote_copy(
            src_ref=placed.at[area], dst_ref=shared.at[slot],
            send_sem=share_send.at[slot], recv_sem=share_recv.at[slot],
            device_id=(sibling, tile), device_id_type=MESH,
        )

    share_far = share(crossed, 0)
    share_far.start()
    share_near = share(sibling, 1)
    share_near.start()

    send_prm.wait()
    gap = (
        lax.broadcasted_iota(jnp.int32, (256, 128), 1)
        - lax.broadcasted_iota(jnp.int32, (256, 128), 0)
        + 128
    ).astype(f32)
    for source in range(2):
        table = prm if source == 0 else sib_prm
        for e in range(2):
            shift = table[pl.ds(4 * e, 1), :]
            frac_row = table[pl.ds(4 * e + 1, 1), :]
            frac_col = table[pl.ds(4 * e + 2, 1), :]
            down = jnp.where(gap == shift, 1.0 - frac_row, 0.0) + jnp.where(
                gap == shift + 1.0, frac_row, 0.0
            )
            for tap in range(2):
                left = down * ((frac_col if tap else 1.0 - frac_col) * (0.5 / math.pi))
                place = (source * 2 + e) * 256 + tap * 128
                for piece in range(PIECES):
                    part = left.astype(bf16)
                    weights[pl.ds(256 * piece, 256), pl.ds(place, 128)] = part
                    left = left - part.astype(f32)

    def fill(slot, k):
        for source in range(2):
            for e in range(2):
                cols = pl.ds(pl.multiple_of(k * CHUNK, CHUNK), CHUNK + 128)
                block = aligned[slot, e, :, cols] if source == 0 else shared[slot, e, :, cols]
                place = (source * 2 + e) * 256
                taps[pl.ds(place, 128), :] = block[:, :CHUNK]
                moved = pltpu.roll(block.astype(f32), CHUNK + 127, 1)
                taps[pl.ds(place + 128, 128), :] = moved[:, :CHUNK].astype(bf16)
        product[...] = jnp.dot(weights[...], taps[...], preferred_element_type=f32)

    def summed(first_row, rows):
        total = product[pl.ds(first_row, rows), :]
        for piece in range(1, PIECES):
            total = total + product[pl.ds(256 * piece + first_row, rows), :]
        return total

    def across(half, k):
        return pltpu.make_async_remote_copy(
            src_ref=x_out.at[half, k], dst_ref=x_in.at[half, k],
            send_sem=x_send.at[half, k], recv_sem=x_recv.at[half, k],
            device_id=(partner, tile), device_id_type=MESH,
        )

    def upward(k):
        return pltpu.make_async_remote_copy(
            src_ref=z_out.at[k], dst_ref=z_in.at[k],
            send_sem=z_send.at[k], recv_sem=z_recv.at[k],
            device_id=(layer, before), device_id_type=MESH,
        )

    loads[0].wait()
    share_far.wait()

    @pl.loop(0, CHUNKS)
    def _(k):
        fill(0, k)
        for block in range(8):
            x_out[block // 4, k, pl.ds(32 * (block % 4), 32), :] = to_link(
                summed(32 * block, 32)
            )
        across(0, k).start()

    @pl.loop(0, CHUNKS)
    def _(k):
        across(1, k).start()

    loads[1].wait()
    share_near.wait()

    @pl.loop(0, CHUNKS)
    def _(k):
        fill(1, k)
        for block in range(8):
            own[block // 4, k, pl.ds(32 * (block % 4), 32), :] = summed(32 * block, 32)

    @pl.loop(0, CHUNKS)
    def _(k):
        across(0, k).wait()
        for block in range(4):
            rows = pl.ds(32 * block, 32)
            z_out[k, rows, :] = to_link(own[0, k, rows, :] + from_link(x_in[0, k, rows, :]))
        upward(k).start()

    loads[2].wait()

    @pl.loop(0, CHUNKS)
    def _(k):
        across(1, k).wait()
        upward(k).wait()
        line = steps[pl.ds(k, 1), :]
        piston = jnp.concatenate([line, line], axis=1)
        sums = [jnp.zeros((8, CHUNK), f32) for _ in range(10)]
        cols = pl.ds(pl.multiple_of(k * CHUNK, CHUNK), CHUNK)
        for block in range(8):
            rows = pl.ds(16 * block, 16)
            turns = (
                own[1, k, rows, :]
                + from_link(x_in[1, k, rows, :])
                + from_link(z_in[k, rows, :])
                + piston
            )
            cos, sin = turn_sincos(turns)
            size = amp[rows, cols].astype(f32)
            real, imag = size * cos, size * sin
            field_re[k, rows, :] = real
            field_im[k, rows, :] = imag
            for base, part in ((0, real), (5, imag)):
                sums[base] = sums[base] + (part[:8] + part[8:])
                for j in range(4):
                    wide = part * rows_t[j, rows, :]
                    sums[base + 1 + j] = sums[base + 1 + j] + (wide[:8] + wide[8:])
        for j in range(10):
            line = jnp.sum(sums[j], axis=0, keepdims=True)
            spread = line * cols_t[:, cols]
            acc[j] = acc[j] + (spread[:, :128] + spread[:, 128:])

    spot = lax.broadcasted_iota(jnp.int32, (8, 128), 1)
    packed = jnp.zeros((8, 128), f32)
    for j in range(10):
        packed = jnp.where(spot == j, jnp.sum(acc[j], axis=1, keepdims=True), packed)
    message[0] = packed

    def exchange(slot, peer, target, sem):
        copies = [
            pltpu.make_async_remote_copy(
                src_ref=message.at[slot], dst_ref=target.at[d],
                send_sem=sem.at[0, d], recv_sem=sem.at[1, d],
                device_id=peer(d), device_id_type=MESH,
            )
            for d in range(1, 16)
        ]
        for copy in copies:
            copy.start()
        total = message[slot]
        for copy in copies:
            copy.wait()
        for d in range(1, 16):
            total = total + target[d]
        return total

    message[1] = exchange(0, near_peer, first, one_sem)
    total = exchange(1, far_peer, second, two_sem)

    row_kind = spot % 5
    col_kind = lax.broadcasted_iota(jnp.int32, (8, 128), 0)
    row_freq = (row_kind + 1) // 2
    col_freq = (col_kind + 1) // 2
    inside = (row_freq * row_freq + col_freq * col_freq <= DOT_RADIUS**2) & (spot < 10)
    factor = (
        jnp.where(inside, 1.0 / (PADDED * PADDED), 0.0)
        * jnp.where(row_kind > 0, 2.0, 1.0)
        * jnp.where(col_kind > 0, 2.0, 1.0)
    )
    turned = jnp.where(spot < 5, -pltpu.roll(total, 123, 1), pltpu.roll(total, 5, 1))
    mix = factor * ((math.cos(phase_step) - 1.0) * total + math.sin(phase_step) * turned)
    for k in range(CHUNKS):
        cols = pl.ds(CHUNK * k, CHUNK)
        lines = [
            jnp.sum(mix[:, j : j + 1] * cols_t[:, cols], axis=0, keepdims=True) for j in range(10)
        ]
        for block in range(8):
            rows = pl.ds(16 * block, 16)
            real = field_re[k, rows, :] + lines[0]
            imag = field_im[k, rows, :] + lines[5]
            for j in range(4):
                table = rows_t[j, rows, :]
                real = real + table * lines[1 + j]
                imag = imag + table * lines[6 + j]
            out[rows, cols] = real * real + imag * imag


def body(screens, chosen, row_shift, column_shift, fractions, pistons, segment_map, amplitude):
    hbm = pl.BlockSpec(memory_space=pltpu.HBM)
    vmem = pl.BlockSpec(memory_space=pltpu.VMEM)
    dma = pltpu.SemaphoreType.DMA
    placed, prm, steps = pl.pallas_call(
        place_kernel,
        out_shape=(
            jax.ShapeDtypeStruct((4, 2, ROWS, WIDE), bf16),
            jax.ShapeDtypeStruct((8, 128), f32),
            jax.ShapeDtypeStruct((8, 128), f32),
        ),
        in_specs=[hbm] * 7,
        out_specs=(hbm, vmem, vmem),
        scratch_shapes=[
            pltpu.SMEM((2,), jnp.int32),
            pltpu.SMEM((2,), jnp.int32),
            pltpu.SMEM((2,), jnp.int32),
            pltpu.SMEM((2, 2), f32),
            pltpu.SMEM(pistons.shape, f32),
            pltpu.SMEM((SEG_GRID, SEG_GRID), jnp.int32),
            pltpu.VMEM((4, 2, ROWS, WIDE), bf16),
            pltpu.VMEM((4, 2, ROWS, WIDE), bf16),
            dma((6,)),
            dma((4, 2)),
            dma((4,)),
        ],
        compiler_params=pltpu.CompilerParams(vmem_limit_bytes=64 * 1024 * 1024),
    )(screens, chosen, row_shift, column_shift, fractions, pistons, segment_map)
    return pl.pallas_call(
        kernel,
        out_shape=jax.ShapeDtypeStruct((ROWS, SHARE), f32),
        in_specs=[hbm, vmem, vmem, hbm],
        out_specs=vmem,
        scratch_shapes=[
            pltpu.VMEM((ROWS, SHARE), bf16),
            pltpu.VMEM((2, 2, ROWS, WIDE), bf16),
            pltpu.VMEM((2, 2, ROWS, WIDE), bf16),
            pltpu.VMEM((8, 128), f32),
            pltpu.VMEM((1024, CHUNK), bf16),
            pltpu.VMEM((256 * PIECES, 1024), bf16),
            pltpu.VMEM((256 * PIECES, CHUNK), f32),
            pltpu.VMEM((2, CHUNKS, ROWS, CHUNK), f32),
            pltpu.VMEM((2, CHUNKS, ROWS, CHUNK), LINK),
            pltpu.VMEM((2, CHUNKS, ROWS, CHUNK), LINK),
            pltpu.VMEM((CHUNKS, ROWS, CHUNK), LINK),
            pltpu.VMEM((CHUNKS, ROWS, CHUNK), LINK),
            pltpu.VMEM((CHUNKS, ROWS, CHUNK), f32),
            pltpu.VMEM((CHUNKS, ROWS, CHUNK), f32),
            pltpu.VMEM((4, ROWS, CHUNK), f32),
            pltpu.VMEM((8, SHARE), f32),
            pltpu.VMEM((10, 8, 128), f32),
            pltpu.VMEM((2, 8, 128), f32),
            pltpu.VMEM((16, 8, 128), f32),
            pltpu.VMEM((16, 8, 128), f32),
            dma((3,)),
            dma((2,)),
            dma((2,)),
            dma((2,)),
            dma((2, CHUNKS)),
            dma((2, CHUNKS)),
            dma((CHUNKS,)),
            dma((CHUNKS,)),
            dma((2, 16)),
            dma((2, 16)),
        ],
        compiler_params=pltpu.CompilerParams(
            collective_id=0, has_side_effects=True, vmem_limit_bytes=64 * 1024 * 1024
        ),
    )(placed, prm, steps, amplitude)


def solution(mesh):
    return jax.shard_map(
        body,
        mesh=mesh,
        in_specs=(
            P("layer", "tile", None),
            P("layer"),
            P("layer"),
            P("layer"),
            P("layer", None),
            P(),
            P(),
            P("tile", None),
        ),
        out_specs=P("tile", "layer"),
        check_vma=False,
    )
```

```python
import functools
import math

import jax
import jax.numpy as jnp
from jax import lax
from jax.experimental import pallas as pl
from jax.experimental.pallas import tpu as pltpu
from jax.sharding import PartitionSpec as P

PUPIL = 8192
PADDED = 16384
SEG_GRID = 32
DOT_RADIUS = 2
ROWS = 128
SHARE = 2048
CHUNK = 256
CHUNKS = SHARE // CHUNK
WIDE = SHARE + 128
PIECES = 2
HALF = CHUNKS // 2
LINK = jnp.bfloat16
SPAN = 500.0
phase_step = math.pi / 2
f32 = jnp.float32
bf16 = jnp.bfloat16
MESH = pl.DeviceIdType.MESH


def nearest(x):
    return jnp.floor(x + 0.5)


def turn_sincos(u):
    r = u - nearest(u)
    q = nearest(4.0 * r)
    x = (r - 0.25 * q) * (2.0 * math.pi)
    z = x * x
    s = x * (1.0 + z * (-1.0 / 6 + z * (1.0 / 120 + z * (-1.0 / 5040 + z * (1.0 / 362880)))))
    c = 1.0 + z * (-0.5 + z * (1.0 / 24 + z * (-1.0 / 720 + z * (1.0 / 40320))))
    odd = jnp.abs(q) == 1.0
    cos = jnp.where(odd, s, c)
    sin = jnp.where(odd, c, s)
    cos = jnp.where((q == 1.0) | (jnp.abs(q) == 2.0), -cos, cos)
    sin = jnp.where((q == -1.0) | (jnp.abs(q) == 2.0), -sin, sin)
    return cos, sin


def to_link(u):
    r = u - nearest(u)
    v = jnp.exp2(jnp.abs(r) * SPAN - 0.25 * SPAN)
    return jnp.where(r < 0.0, -v, v).astype(LINK)


def from_link(v):
    v = v.astype(f32)
    r = jnp.log(jnp.abs(v)) * (1.0 / (math.log(2.0) * SPAN)) + 0.25
    return jnp.where(v < 0.0, -r, r)


def place_kernel(
    screens, chosen_hbm, row_shift_hbm, column_shift_hbm, fractions_hbm, pistons_hbm, map_hbm,
    aligned, prm, steps,
    chosen, column_shift, row_shift, fractions, pistons, segment_map,
    raw, ready, small_sem, load_sem, store_sem,
):
    small = [
        pltpu.make_async_copy(source, target, small_sem.at[i])
        for i, (source, target) in enumerate(
            (
                (chosen_hbm, chosen),
                (column_shift_hbm, column_shift),
                (row_shift_hbm, row_shift),
                (fractions_hbm, fractions),
                (pistons_hbm, pistons),
                (map_hbm, segment_map),
            )
        )
    ]
    for copy in small:
        copy.start()
    layer = lax.axis_index("layer")
    tile = lax.axis_index("tile")
    sibling = (layer // 2) * 2 + 1 - layer % 2
    order = ((sibling + 2) % 4, (layer + 2) % 4, sibling, layer)

    def load(area, e):
        start = (column_shift[e] // 128 + 16 * area) * 128
        return pltpu.make_async_copy(
            screens.at[chosen[e], :, pl.ds(pl.multiple_of(start, 128), WIDE)],
            raw.at[area, e],
            load_sem.at[area, e],
        )

    def store(area):
        return pltpu.make_async_copy(ready.at[area], aligned.at[area], store_sem.at[area])

    for copy in small[:2]:
        copy.wait()
    for area in order:
        for e in range(2):
            load(area, e).start()
    for copy in small[2:]:
        copy.wait()
    for e in range(2):
        prm[pl.ds(4 * e, 1), :] = jnp.full((1, 128), row_shift[e], jnp.int32).astype(f32)
        prm[pl.ds(4 * e + 1, 1), :] = jnp.full((1, 128), fractions[e, 0], f32)
        prm[pl.ds(4 * e + 2, 1), :] = jnp.full((1, 128), fractions[e, 1], f32)
        prm[pl.ds(4 * e + 3, 1), :] = jnp.zeros((1, 128), f32)
    for k in range(CHUNKS):
        piston = pistons[segment_map[tile // 2, layer * CHUNKS + k]]
        steps[pl.ds(k, 1), :] = jnp.full((1, 128), piston * (0.5 / math.pi), f32)
    lane = lax.broadcasted_iota(jnp.int32, (ROWS, 128), 1)
    for area in order:
        for e in range(2):
            load(area, e).wait()
            part = column_shift[e] % 128
            keep = lane < 128 - part

            def rolled(j):
                block = raw[area, e, :, pl.ds(128 * j, 128)].astype(f32)
                return pltpu.roll(block, (128 - part) % 128, 1)

            previous = rolled(0)
            for j in range(16):
                following = rolled(j + 1)
                ready[area, e, :, pl.ds(128 * j, 128)] = jnp.where(
                    keep, previous, following
                ).astype(bf16)
                previous = following
            ready[area, e, :, pl.ds(SHARE, 128)] = previous.astype(bf16)
        store(area).start()
    for area in order:
        store(area).wait()


def kernel(
    placed, prm, steps, amplitude, out,
    amp, aligned, shared, sib_prm, taps, weights, product, own,
    x_out, x_in, z_out, z_in, p_out, p_in, held,
    field_re, field_im, rows_t, cols_t, acc, message, arrived,
    load_sem, share_send, share_recv, prm_sem, x_send, x_recv, z_send, z_recv,
    p_send, p_recv, sum_sem,
):
    layer = lax.axis_index("layer")
    tile = lax.axis_index("tile")
    pair, core = layer // 2, layer % 2
    sibling = pair * 2 + 1 - core
    partner = (1 - pair) * 2 + core
    crossed = (1 - pair) * 2 + 1 - core
    before = (tile + 63) % 64
    after = (tile + 1) % 64

    x = (tile // 32) * 2 + pair
    y = (tile // 8) % 4
    z = tile % 8

    def at(x, y, z, core):
        return (x % 2) * 2 + core, (x // 2) * 32 + y * 8 + z

    def z_peer(d):
        return at(x, y, (z + d) % 8, core)

    def y_peer(d):
        place = (y * 2 + core + d) % 8
        return at(x, place // 2, z, place % 2)

    def x_peer(d):
        return at((x + d) % 4, y, z, core)

    stages = ((8, z_peer), (8, y_peer), (4, x_peer))

    loads = [
        pltpu.make_async_copy(placed.at[area], aligned.at[slot], load_sem.at[slot])
        for slot, area in enumerate((partner, layer))
    ]
    loads.append(
        pltpu.make_async_copy(
            amplitude.at[:, pl.ds(pl.multiple_of(layer * SHARE, SHARE), SHARE)],
            amp,
            load_sem.at[2],
        )
    )
    for load in loads:
        load.start()

    barrier = pltpu.get_barrier_semaphore()
    greeted = [(sibling, tile), (layer, before), (layer, after)]
    greeted += [peer(d) for size, peer in stages for d in range(1, size)]
    for device in greeted:
        pl.semaphore_signal(barrier, inc=1, device_id=device, device_id_type=MESH)

    row_id = lax.broadcasted_iota(jnp.int32, (ROWS, 128), 0) + tile * ROWS
    for k in (1, 2):
        cos, sin = turn_sincos((row_id * k).astype(f32) * (1.0 / PADDED))
        for half in range(2):
            rows_t[2 * k - 2, :, pl.ds(128 * half, 128)] = cos
            rows_t[2 * k - 1, :, pl.ds(128 * half, 128)] = sin
    kind = lax.broadcasted_iota(jnp.int32, (8, SHARE), 0)
    col_id = lax.broadcasted_iota(jnp.int32, (8, SHARE), 1) + layer * SHARE
    cos, sin = turn_sincos((col_id * ((kind + 1) // 2)).astype(f32) * (1.0 / PADDED))
    table = jnp.where((kind == 2) | (kind == 4), sin, cos)
    cols_t[...] = jnp.where(kind < 5, table, 0.0)
    acc[...] = jnp.zeros_like(acc)

    pl.semaphore_wait(barrier, len(greeted))
    send_prm = pltpu.make_async_remote_copy(
        src_ref=prm, dst_ref=sib_prm, send_sem=prm_sem.at[0], recv_sem=prm_sem.at[1],
        device_id=(sibling, tile), device_id_type=MESH,
    )
    send_prm.start()
    def share(area, slot):
        return pltpu.make_async_remote_copy(
            src_ref=placed.at[area], dst_ref=shared.at[slot],
            send_sem=share_send.at[slot], recv_sem=share_recv.at[slot],
            device_id=(sibling, tile), device_id_type=MESH,
        )

    share_far = share(crossed, 0)
    share_far.start()
    share_near = share(sibling, 1)
    share_near.start()

    send_prm.wait()
    gap = (
        lax.broadcasted_iota(jnp.int32, (256, 128), 1)
        - lax.broadcasted_iota(jnp.int32, (256, 128), 0)
        + 128
    ).astype(f32)
    for source in range(2):
        table = prm if source == 0 else sib_prm
        for e in range(2):
            shift = table[pl.ds(4 * e, 1), :]
            frac_row = table[pl.ds(4 * e + 1, 1), :]
            frac_col = table[pl.ds(4 * e + 2, 1), :]
            down = jnp.where(gap == shift, 1.0 - frac_row, 0.0) + jnp.where(
                gap == shift + 1.0, frac_row, 0.0
            )
            for tap in range(2):
                left = down * ((frac_col if tap else 1.0 - frac_col) * (0.5 / math.pi))
                place = (source * 2 + e) * 256 + tap * 128
                for piece in range(PIECES):
                    part = left.astype(bf16)
                    weights[pl.ds(256 * piece, 256), pl.ds(place, 128)] = part
                    left = left - part.astype(f32)

    def fill(slot, k):
        for source in range(2):
            for e in range(2):
                cols = pl.ds(pl.multiple_of(k * CHUNK, CHUNK), CHUNK + 128)
                block = aligned[slot, e, :, cols] if source == 0 else shared[slot, e, :, cols]
                place = (source * 2 + e) * 256
                taps[pl.ds(place, 128), :] = block[:, :CHUNK]
                moved = pltpu.roll(block.astype(f32), CHUNK + 127, 1)
                taps[pl.ds(place + 128, 128), :] = moved[:, :CHUNK].astype(bf16)
        product[...] = jnp.dot(weights[...], taps[...], preferred_element_type=f32)

    def summed(first_row, rows):
        total = product[pl.ds(first_row, rows), :]
        for piece in range(1, PIECES):
            total = total + product[pl.ds(256 * piece + first_row, rows), :]
        return total

    def across(half, k):
        return pltpu.make_async_remote_copy(
            src_ref=x_out.at[half, k], dst_ref=x_in.at[half, k],
            send_sem=x_send.at[half, k], recv_sem=x_recv.at[half, k],
            device_id=(partner, tile), device_id_type=MESH,
        )

    def upward(k):
        return pltpu.make_async_remote_copy(
            src_ref=z_out.at[k], dst_ref=z_in.at[k],
            send_sem=z_send.at[k], recv_sem=z_recv.at[k],
            device_id=(layer, before), device_id_type=MESH,
        )

    def upward_first(k):
        return pltpu.make_async_remote_copy(
            src_ref=p_out.at[k], dst_ref=p_in.at[k],
            send_sem=p_send.at[k], recv_sem=p_recv.at[k],
            device_id=(layer, before), device_id_type=MESH,
        )

    quarters = [pl.ds(32 * block, 32) for block in range(4)]

    def relay(i):
        upward_first(i).wait_recv()
        for rows in quarters:
            x_out[1, i, rows, :] = to_link(held[i, rows, :] + from_link(p_in[i, rows, :]))
        across(1, i).start()
        k = i + HALF
        across(0, k).wait_recv()
        for rows in quarters:
            z_out[k, rows, :] = to_link(own[0, k, rows, :] + from_link(x_in[0, k, rows, :]))
        upward(k).start()

    loads[0].wait()
    share_far.wait()
    loads[1].wait()
    share_near.wait()

    @pl.loop(0, HALF)
    def _(i):
        k = i + HALF
        fill(0, k)
        for half in range(2):
            for block, rows in enumerate(quarters):
                x_out[half, k, rows, :] = to_link(summed(128 * half + 32 * block, 32))
            across(half, k).start()
        fill(0, i)
        for block, rows in enumerate(quarters):
            p_out[i, rows, :] = to_link(summed(32 * block, 32))
        upward_first(i).start()
        for block, rows in enumerate(quarters):
            held[i, rows, :] = summed(128 + 32 * block, 32)
        fill(1, i)
        for block, rows in enumerate(quarters):
            z_out[i, rows, :] = to_link(summed(32 * block, 32))
        upward(i).start()
        for block, rows in enumerate(quarters):
            own[1, i, rows, :] = summed(128 + 32 * block, 32)
        fill(1, k)
        for half in range(2):
            for block, rows in enumerate(quarters):
                own[half, k, rows, :] = summed(128 * half + 32 * block, 32)

        @pl.when(i >= 1)
        def _():
            relay(i - 1)

    relay(HALF - 1)
    loads[2].wait()

    @pl.loop(0, CHUNKS)
    def _(i):
        k = i // 2 + HALF * (1 - i % 2)
        across(1, k).wait_recv()
        upward(k).wait_recv()
        line = steps[pl.ds(k, 1), :]
        piston = jnp.concatenate([line, line], axis=1)
        sums = [jnp.zeros((8, CHUNK), f32) for _ in range(10)]
        cols = pl.ds(pl.multiple_of(k * CHUNK, CHUNK), CHUNK)
        for block in range(8):
            rows = pl.ds(16 * block, 16)
            turns = (
                own[1, k, rows, :]
                + from_link(x_in[1, k, rows, :])
                + from_link(z_in[k, rows, :])
                + piston
            )
            cos, sin = turn_sincos(turns)
            size = amp[rows, cols].astype(f32)
            real, imag = size * cos, size * sin
            field_re[k, rows, :] = real
            field_im[k, rows, :] = imag
            for base, part in ((0, real), (5, imag)):
                sums[base] = sums[base] + (part[:8] + part[8:])
                for j in range(4):
                    wide = part * rows_t[j, rows, :]
                    sums[base + 1 + j] = sums[base + 1 + j] + (wide[:8] + wide[8:])
        for j in range(10):
            line = jnp.sum(sums[j], axis=0, keepdims=True)
            spread = line * cols_t[:, cols]
            acc[j] = acc[j] + (spread[:, :128] + spread[:, 128:])

    spot = lax.broadcasted_iota(jnp.int32, (8, 128), 1)
    packed = jnp.zeros((8, 128), f32)
    for j in range(10):
        packed = jnp.where(spot == j, jnp.sum(acc[j], axis=1, keepdims=True), packed)
    total = packed
    sent = []
    for stage, (size, peer) in enumerate(stages):
        message[stage] = total
        copies = [
            pltpu.make_async_remote_copy(
                src_ref=message.at[stage], dst_ref=arrived.at[stage, d],
                send_sem=sum_sem.at[0, stage, d], recv_sem=sum_sem.at[1, stage, d],
                device_id=peer(d), device_id_type=MESH,
            )
            for d in range(1, size)
        ]
        for copy in copies:
            copy.start()
        for d, copy in enumerate(copies):
            copy.wait_recv()
            total = total + arrived[stage, d + 1]
        sent += copies

    row_kind = spot % 5
    col_kind = lax.broadcasted_iota(jnp.int32, (8, 128), 0)
    row_freq = (row_kind + 1) // 2
    col_freq = (col_kind + 1) // 2
    inside = (row_freq * row_freq + col_freq * col_freq <= DOT_RADIUS**2) & (spot < 10)
    factor = (
        jnp.where(inside, 1.0 / (PADDED * PADDED), 0.0)
        * jnp.where(row_kind > 0, 2.0, 1.0)
        * jnp.where(col_kind > 0, 2.0, 1.0)
    )
    turned = jnp.where(spot < 5, -pltpu.roll(total, 123, 1), pltpu.roll(total, 5, 1))
    mix = factor * ((math.cos(phase_step) - 1.0) * total + math.sin(phase_step) * turned)
    for k in range(CHUNKS):
        cols = pl.ds(CHUNK * k, CHUNK)
        lines = [
            jnp.sum(mix[:, j : j + 1] * cols_t[:, cols], axis=0, keepdims=True) for j in range(10)
        ]
        for block in range(8):
            rows = pl.ds(16 * block, 16)
            real = field_re[k, rows, :] + lines[0]
            imag = field_im[k, rows, :] + lines[5]
            for j in range(4):
                table = rows_t[j, rows, :]
                real = real + table * lines[1 + j]
                imag = imag + table * lines[6 + j]
            out[rows, cols] = real * real + imag * imag

    for copy in sent:
        copy.wait_send()
    for k in range(CHUNKS):
        upward(k).wait_send()
        across(1, k).wait_send()
    for k in range(HALF):
        upward_first(k).wait_send()
        across(0, k + HALF).wait_send()


def body(screens, chosen, row_shift, column_shift, fractions, pistons, segment_map, amplitude):
    hbm = pl.BlockSpec(memory_space=pltpu.HBM)
    vmem = pl.BlockSpec(memory_space=pltpu.VMEM)
    dma = pltpu.SemaphoreType.DMA
    placed, prm, steps = pl.pallas_call(
        place_kernel,
        out_shape=(
            jax.ShapeDtypeStruct((4, 2, ROWS, WIDE), bf16),
            jax.ShapeDtypeStruct((8, 128), f32),
            jax.ShapeDtypeStruct((8, 128), f32),
        ),
        in_specs=[hbm] * 7,
        out_specs=(hbm, vmem, vmem),
        scratch_shapes=[
            pltpu.SMEM((2,), jnp.int32),
            pltpu.SMEM((2,), jnp.int32),
            pltpu.SMEM((2,), jnp.int32),
            pltpu.SMEM((2, 2), f32),
            pltpu.SMEM(pistons.shape, f32),
            pltpu.SMEM((SEG_GRID, SEG_GRID), jnp.int32),
            pltpu.VMEM((4, 2, ROWS, WIDE), bf16),
            pltpu.VMEM((4, 2, ROWS, WIDE), bf16),
            dma((6,)),
            dma((4, 2)),
            dma((4,)),
        ],
        compiler_params=pltpu.CompilerParams(vmem_limit_bytes=64 * 1024 * 1024),
    )(screens, chosen, row_shift, column_shift, fractions, pistons, segment_map)
    return pl.pallas_call(
        kernel,
        out_shape=jax.ShapeDtypeStruct((ROWS, SHARE), f32),
        in_specs=[hbm, vmem, vmem, hbm],
        out_specs=vmem,
        scratch_shapes=[
            pltpu.VMEM((ROWS, SHARE), bf16),
            pltpu.VMEM((2, 2, ROWS, WIDE), bf16),
            pltpu.VMEM((2, 2, ROWS, WIDE), bf16),
            pltpu.VMEM((8, 128), f32),
            pltpu.VMEM((1024, CHUNK), bf16),
            pltpu.VMEM((256 * PIECES, 1024), bf16),
            pltpu.VMEM((256 * PIECES, CHUNK), f32),
            pltpu.VMEM((2, CHUNKS, ROWS, CHUNK), f32),
            pltpu.VMEM((2, CHUNKS, ROWS, CHUNK), LINK),
            pltpu.VMEM((2, CHUNKS, ROWS, CHUNK), LINK),
            pltpu.VMEM((CHUNKS, ROWS, CHUNK), LINK),
            pltpu.VMEM((CHUNKS, ROWS, CHUNK), LINK),
            pltpu.VMEM((HALF, ROWS, CHUNK), LINK),
            pltpu.VMEM((HALF, ROWS, CHUNK), LINK),
            pltpu.VMEM((HALF, ROWS, CHUNK), f32),
            pltpu.VMEM((CHUNKS, ROWS, CHUNK), f32),
            pltpu.VMEM((CHUNKS, ROWS, CHUNK), f32),
            pltpu.VMEM((4, ROWS, CHUNK), f32),
            pltpu.VMEM((8, SHARE), f32),
            pltpu.VMEM((10, 8, 128), f32),
            pltpu.VMEM((3, 8, 128), f32),
            pltpu.VMEM((3, 8, 8, 128), f32),
            dma((3,)),
            dma((2,)),
            dma((2,)),
            dma((2,)),
            dma((2, CHUNKS)),
            dma((2, CHUNKS)),
            dma((CHUNKS,)),
            dma((CHUNKS,)),
            dma((HALF,)),
            dma((HALF,)),
            dma((2, 3, 8)),
        ],
        compiler_params=pltpu.CompilerParams(
            collective_id=0, has_side_effects=True, vmem_limit_bytes=64 * 1024 * 1024
        ),
    )(placed, prm, steps, amplitude)


def solution(mesh):
    return jax.shard_map(
        body,
        mesh=mesh,
        in_specs=(
            P("layer", "tile", None),
            P("layer"),
            P("layer"),
            P("layer"),
            P("layer", None),
            P(),
            P(),
            P("tile", None),
        ),
        out_specs=P("tile", "layer"),
        check_vma=False,
    )
```

```python
import functools
import math

import jax
import jax.numpy as jnp
from jax import lax
from jax.experimental import pallas as pl
from jax.experimental.pallas import tpu as pltpu
from jax.sharding import PartitionSpec as P

PUPIL = 8192
PADDED = 16384
SEG_GRID = 32
DOT_RADIUS = 2
ROWS = 128
SHARE = 2048
CHUNK = 256
CHUNKS = SHARE // CHUNK
WIDE = SHARE + 128
PIECES = 2
HALF = CHUNKS // 2
LINK = jnp.bfloat16
SPAN = 500.0
phase_step = math.pi / 2
f32 = jnp.float32
bf16 = jnp.bfloat16
MESH = pl.DeviceIdType.MESH


def nearest(x):
    return jnp.floor(x + 0.5)


def turn_sincos(u):
    r = u - nearest(u)
    q = nearest(4.0 * r)
    x = (r - 0.25 * q) * (2.0 * math.pi)
    z = x * x
    s = x * (1.0 + z * (-1.0 / 6 + z * (1.0 / 120 + z * (-1.0 / 5040 + z * (1.0 / 362880)))))
    c = 1.0 + z * (-0.5 + z * (1.0 / 24 + z * (-1.0 / 720 + z * (1.0 / 40320))))
    odd = jnp.abs(q) == 1.0
    cos = jnp.where(odd, s, c)
    sin = jnp.where(odd, c, s)
    cos = jnp.where((q == 1.0) | (jnp.abs(q) == 2.0), -cos, cos)
    sin = jnp.where((q == -1.0) | (jnp.abs(q) == 2.0), -sin, sin)
    return cos, sin


def to_link(u):
    r = u - nearest(u)
    v = jnp.exp2(jnp.abs(r) * SPAN - 0.25 * SPAN)
    return jnp.where(r < 0.0, -v, v).astype(LINK)


def from_link(v):
    v = v.astype(f32)
    r = jnp.log(jnp.abs(v)) * (1.0 / (math.log(2.0) * SPAN)) + 0.25
    return jnp.where(v < 0.0, -r, r)


def place_kernel(
    screens, chosen_hbm, row_shift_hbm, column_shift_hbm, fractions_hbm, pistons_hbm, map_hbm,
    aligned, prm, steps,
    chosen, column_shift, row_shift, fractions, pistons, segment_map,
    raw, ready, small_sem, load_sem, store_sem,
):
    small = [
        pltpu.make_async_copy(source, target, small_sem.at[i])
        for i, (source, target) in enumerate(
            (
                (chosen_hbm, chosen),
                (column_shift_hbm, column_shift),
                (row_shift_hbm, row_shift),
                (fractions_hbm, fractions),
                (pistons_hbm, pistons),
                (map_hbm, segment_map),
            )
        )
    ]
    for copy in small:
        copy.start()
    layer = lax.axis_index("layer")
    tile = lax.axis_index("tile")
    sibling = (layer // 2) * 2 + 1 - layer % 2
    order = ((sibling + 2) % 4, (layer + 2) % 4, sibling, layer)

    def load(area, e):
        start = (column_shift[e] // 128 + 16 * area) * 128
        return pltpu.make_async_copy(
            screens.at[chosen[e], :, pl.ds(pl.multiple_of(start, 128), WIDE)],
            raw.at[area, e],
            load_sem.at[area, e],
        )

    def store(area):
        return pltpu.make_async_copy(ready.at[area], aligned.at[area], store_sem.at[area])

    for copy in small[:2]:
        copy.wait()
    for area in order:
        for e in range(2):
            load(area, e).start()
    for copy in small[2:]:
        copy.wait()
    for e in range(2):
        prm[pl.ds(4 * e, 1), :] = jnp.full((1, 128), row_shift[e], jnp.int32).astype(f32)
        prm[pl.ds(4 * e + 1, 1), :] = jnp.full((1, 128), fractions[e, 0], f32)
        prm[pl.ds(4 * e + 2, 1), :] = jnp.full((1, 128), fractions[e, 1], f32)
        prm[pl.ds(4 * e + 3, 1), :] = jnp.zeros((1, 128), f32)
    for k in range(CHUNKS):
        piston = pistons[segment_map[tile // 2, layer * CHUNKS + k]]
        steps[pl.ds(k, 1), :] = jnp.full((1, 128), piston * (0.5 / math.pi), f32)
    lane = lax.broadcasted_iota(jnp.int32, (ROWS, 128), 1)
    for area in order:
        for e in range(2):
            load(area, e).wait()
            part = column_shift[e] % 128
            keep = lane < 128 - part

            def rolled(j):
                block = raw[area, e, :, pl.ds(128 * j, 128)].astype(f32)
                return pltpu.roll(block, (128 - part) % 128, 1)

            previous = rolled(0)
            for j in range(16):
                following = rolled(j + 1)
                ready[area, e, :, pl.ds(128 * j, 128)] = jnp.where(
                    keep, previous, following
                ).astype(bf16)
                previous = following
            ready[area, e, :, pl.ds(SHARE, 128)] = previous.astype(bf16)
        store(area).start()
    for area in order:
        store(area).wait()


def kernel(
    placed, prm, steps, amplitude, out,
    amp, aligned, shared, sib_prm, taps, weights, product, own,
    x_out, x_in, z_out, z_in, p_out, p_in, held, lows,
    field_re, field_im, rows_t, cols_t, acc, message, arrived,
    load_sem, share_send, share_recv, prm_sem, x_send, x_recv, z_send, z_recv,
    p_send, p_recv, sum_sem,
):
    layer = lax.axis_index("layer")
    tile = lax.axis_index("tile")
    pair, core = layer // 2, layer % 2
    sibling = pair * 2 + 1 - core
    partner = (1 - pair) * 2 + core
    crossed = (1 - pair) * 2 + 1 - core
    before = (tile + 63) % 64
    after = (tile + 1) % 64

    flip = (tile % 32 == 0).astype(jnp.int32)
    target = jnp.where(tile % 32 == 0, partner, layer)
    origin = jnp.where(tile % 32 == 31, partner, layer)
    x = (tile // 32) * 2 + pair
    y = (tile // 8) % 4
    z = tile % 8

    def at(x, y, z, core):
        return (x % 2) * 2 + core, (x // 2) * 32 + y * 8 + z

    def z_peer(d):
        return at(x, y, (z + d) % 8, core)

    def y_peer(d):
        place = (y * 2 + core + d) % 8
        return at(x, place // 2, z, place % 2)

    def x_peer(d):
        return at((x + d) % 4, y, z, core)

    def near_peer(d):
        place = (z * 2 + core + d) % 16
        return at(x, y, place // 2, place % 2)

    def far_peer(d):
        place = (y * 4 + x + d) % 16
        return at(place % 4, place // 4, z, core)

    stages = ((16, near_peer), (16, far_peer))

    loads = [
        pltpu.make_async_copy(placed.at[area], aligned.at[slot], load_sem.at[slot])
        for slot, area in enumerate((partner, layer))
    ]
    loads.append(
        pltpu.make_async_copy(
            amplitude.at[:, pl.ds(pl.multiple_of(layer * SHARE, SHARE), SHARE)],
            amp,
            load_sem.at[2],
        )
    )
    for load in loads:
        load.start()

    barrier = pltpu.get_barrier_semaphore()
    greeted = [(sibling, tile), (target, before), (origin, after)]
    greeted += [peer(d) for size, peer in stages for d in range(1, size)]
    for device in greeted:
        pl.semaphore_signal(barrier, inc=1, device_id=device, device_id_type=MESH)

    row_id = lax.broadcasted_iota(jnp.int32, (ROWS, 128), 0) + tile * ROWS
    for k in (1, 2):
        cos, sin = turn_sincos((row_id * k).astype(f32) * (1.0 / PADDED))
        for half in range(2):
            rows_t[2 * k - 2, :, pl.ds(128 * half, 128)] = cos
            rows_t[2 * k - 1, :, pl.ds(128 * half, 128)] = sin
    kind = lax.broadcasted_iota(jnp.int32, (8, SHARE), 0)
    col_id = lax.broadcasted_iota(jnp.int32, (8, SHARE), 1) + layer * SHARE
    cos, sin = turn_sincos((col_id * ((kind + 1) // 2)).astype(f32) * (1.0 / PADDED))
    table = jnp.where((kind == 2) | (kind == 4), sin, cos)
    cols_t[...] = jnp.where(kind < 5, table, 0.0)
    acc[...] = jnp.zeros_like(acc)

    pl.semaphore_wait(barrier, len(greeted))
    send_prm = pltpu.make_async_remote_copy(
        src_ref=prm, dst_ref=sib_prm, send_sem=prm_sem.at[0], recv_sem=prm_sem.at[1],
        device_id=(sibling, tile), device_id_type=MESH,
    )
    send_prm.start()
    def share(area, slot):
        return pltpu.make_async_remote_copy(
            src_ref=placed.at[area], dst_ref=shared.at[slot],
            send_sem=share_send.at[slot], recv_sem=share_recv.at[slot],
            device_id=(sibling, tile), device_id_type=MESH,
        )

    share_far = share(crossed, 0)
    share_far.start()
    share_near = share(sibling, 1)
    share_near.start()

    send_prm.wait()
    gap = (
        lax.broadcasted_iota(jnp.int32, (256, 128), 1)
        - lax.broadcasted_iota(jnp.int32, (256, 128), 0)
        + 128
    ).astype(f32)
    for source in range(2):
        table = prm if source == 0 else sib_prm
        for e in range(2):
            shift = table[pl.ds(4 * e, 1), :]
            frac_row = table[pl.ds(4 * e + 1, 1), :]
            frac_col = table[pl.ds(4 * e + 2, 1), :]
            down = jnp.where(gap == shift, 1.0 - frac_row, 0.0) + jnp.where(
                gap == shift + 1.0, frac_row, 0.0
            )
            for tap in range(2):
                left = down * ((frac_col if tap else 1.0 - frac_col) * (0.5 / math.pi))
                place = (source * 2 + e) * 256 + tap * 128
                for piece in range(PIECES):
                    part = left.astype(bf16)
                    weights[pl.ds(256 * piece, 256), pl.ds(place, 128)] = part
                    left = left - part.astype(f32)

    def fill(slot, k):
        for source in range(2):
            for e in range(2):
                cols = pl.ds(pl.multiple_of(k * CHUNK, CHUNK), CHUNK + 128)
                block = aligned[slot, e, :, cols] if source == 0 else shared[slot, e, :, cols]
                place = (source * 2 + e) * 256
                taps[pl.ds(place, 128), :] = block[:, :CHUNK]
                moved = pltpu.roll(block.astype(f32), CHUNK + 127, 1)
                taps[pl.ds(place + 128, 128), :] = moved[:, :CHUNK].astype(bf16)
        product[...] = jnp.dot(weights[...], taps[...], preferred_element_type=f32)

    def summed(first_row, rows):
        total = product[pl.ds(first_row, rows), :]
        for piece in range(1, PIECES):
            total = total + product[pl.ds(256 * piece + first_row, rows), :]
        return total

    def across(half, k):
        return pltpu.make_async_remote_copy(
            src_ref=x_out.at[half, k], dst_ref=x_in.at[half, k],
            send_sem=x_send.at[half, k], recv_sem=x_recv.at[half, k],
            device_id=(partner, tile), device_id_type=MESH,
        )

    def upward(k):
        return pltpu.make_async_remote_copy(
            src_ref=z_out.at[k], dst_ref=z_in.at[k],
            send_sem=z_send.at[k], recv_sem=z_recv.at[k],
            device_id=(target, before), device_id_type=MESH,
        )

    def upward_first(k):
        return pltpu.make_async_remote_copy(
            src_ref=p_out.at[k], dst_ref=p_in.at[k],
            send_sem=p_send.at[k], recv_sem=p_recv.at[k],
            device_id=(target, before), device_id_type=MESH,
        )

    quarters = [pl.ds(32 * block, 32) for block in range(4)]

    def relay(i):
        upward_first(i).wait_recv()
        for rows in quarters:
            x_out[1, i, rows, :] = to_link(held[i, rows, :] + from_link(p_in[i, rows, :]))
        across(1, i).start()
        k = i + HALF
        across(0, k).wait_recv()
        for rows in quarters:
            z_out[k, rows, :] = to_link(
                lows[1 - flip, k, rows, :] + from_link(x_in[0, k, rows, :])
            )
        upward(k).start()

    loads[0].wait()
    share_far.wait()
    loads[1].wait()
    share_near.wait()

    @pl.loop(0, HALF)
    def _(i):
        k = i + HALF
        def sums(slot, k, target, index, convert):
            fill(slot, k)
            for block, rows in enumerate(quarters):
                target[(*index, rows, slice(None))] = convert(summed(128 + 32 * block, 32))
                lows[slot, k, rows, :] = summed(32 * block, 32)

        sums(0, k, x_out, (1, k), to_link)
        across(1, k).start()
        sums(1, k, own, (k,), lambda v: v)
        for rows in quarters:
            x_out[0, k, rows, :] = to_link(lows[flip, k, rows, :])
        across(0, k).start()
        sums(0, i, held, (i,), lambda v: v)
        sums(1, i, own, (i,), lambda v: v)
        for rows in quarters:
            p_out[i, rows, :] = to_link(lows[flip, i, rows, :])
        upward_first(i).start()
        for rows in quarters:
            z_out[i, rows, :] = to_link(lows[1 - flip, i, rows, :])
        upward(i).start()

        @pl.when(i >= 1)
        def _():
            relay(i - 1)

    relay(HALF - 1)
    loads[2].wait()

    @pl.loop(0, CHUNKS)
    def _(i):
        k = i // 2 + HALF * (1 - i % 2)
        across(1, k).wait_recv()
        upward(k).wait_recv()
        line = steps[pl.ds(k, 1), :]
        piston = jnp.concatenate([line, line], axis=1)
        sums = [jnp.zeros((8, CHUNK), f32) for _ in range(10)]
        cols = pl.ds(pl.multiple_of(k * CHUNK, CHUNK), CHUNK)
        for block in range(8):
            rows = pl.ds(16 * block, 16)
            turns = (
                own[k, rows, :]
                + from_link(x_in[1, k, rows, :])
                + from_link(z_in[k, rows, :])
                + piston
            )
            cos, sin = turn_sincos(turns)
            size = amp[rows, cols].astype(f32)
            real, imag = size * cos, size * sin
            field_re[k, rows, :] = real
            field_im[k, rows, :] = imag
            for base, part in ((0, real), (5, imag)):
                sums[base] = sums[base] + (part[:8] + part[8:])
                for j in range(4):
                    wide = part * rows_t[j, rows, :]
                    sums[base + 1 + j] = sums[base + 1 + j] + (wide[:8] + wide[8:])
        for j in range(10):
            line = jnp.sum(sums[j], axis=0, keepdims=True)
            spread = line * cols_t[:, cols]
            acc[j] = acc[j] + (spread[:, :128] + spread[:, 128:])

    spot = lax.broadcasted_iota(jnp.int32, (8, 128), 1)
    packed = jnp.zeros((8, 128), f32)
    for j in range(10):
        packed = jnp.where(spot == j, jnp.sum(acc[j], axis=1, keepdims=True), packed)
    total = packed
    sent = []
    for stage, (size, peer) in enumerate(stages):
        message[stage] = total
        copies = [
            pltpu.make_async_remote_copy(
                src_ref=message.at[stage], dst_ref=arrived.at[stage, d],
                send_sem=sum_sem.at[0, stage, d], recv_sem=sum_sem.at[1, stage, d],
                device_id=peer(d), device_id_type=MESH,
            )
            for d in range(1, size)
        ]
        for copy in copies:
            copy.start()
        for d, copy in enumerate(copies):
            copy.wait_recv()
            total = total + arrived[stage, d + 1]
        sent += copies

    row_kind = spot % 5
    col_kind = lax.broadcasted_iota(jnp.int32, (8, 128), 0)
    row_freq = (row_kind + 1) // 2
    col_freq = (col_kind + 1) // 2
    inside = (row_freq * row_freq + col_freq * col_freq <= DOT_RADIUS**2) & (spot < 10)
    factor = (
        jnp.where(inside, 1.0 / (PADDED * PADDED), 0.0)
        * jnp.where(row_kind > 0, 2.0, 1.0)
        * jnp.where(col_kind > 0, 2.0, 1.0)
    )
    turned = jnp.where(spot < 5, -pltpu.roll(total, 123, 1), pltpu.roll(total, 5, 1))
    mix = factor * ((math.cos(phase_step) - 1.0) * total + math.sin(phase_step) * turned)
    for k in range(CHUNKS):
        cols = pl.ds(CHUNK * k, CHUNK)
        lines = [
            jnp.sum(mix[:, j : j + 1] * cols_t[:, cols], axis=0, keepdims=True) for j in range(10)
        ]
        for block in range(8):
            rows = pl.ds(16 * block, 16)
            real = field_re[k, rows, :] + lines[0]
            imag = field_im[k, rows, :] + lines[5]
            for j in range(4):
                table = rows_t[j, rows, :]
                real = real + table * lines[1 + j]
                imag = imag + table * lines[6 + j]
            out[rows, cols] = real * real + imag * imag

    for copy in sent:
        copy.wait_send()
    for k in range(CHUNKS):
        upward(k).wait_send()
        across(1, k).wait_send()
    for k in range(HALF):
        upward_first(k).wait_send()
        across(0, k + HALF).wait_send()


def body(screens, chosen, row_shift, column_shift, fractions, pistons, segment_map, amplitude):
    hbm = pl.BlockSpec(memory_space=pltpu.HBM)
    vmem = pl.BlockSpec(memory_space=pltpu.VMEM)
    dma = pltpu.SemaphoreType.DMA
    placed, prm, steps = pl.pallas_call(
        place_kernel,
        out_shape=(
            jax.ShapeDtypeStruct((4, 2, ROWS, WIDE), bf16),
            jax.ShapeDtypeStruct((8, 128), f32),
            jax.ShapeDtypeStruct((8, 128), f32),
        ),
        in_specs=[hbm] * 7,
        out_specs=(hbm, vmem, vmem),
        scratch_shapes=[
            pltpu.SMEM((2,), jnp.int32),
            pltpu.SMEM((2,), jnp.int32),
            pltpu.SMEM((2,), jnp.int32),
            pltpu.SMEM((2, 2), f32),
            pltpu.SMEM(pistons.shape, f32),
            pltpu.SMEM((SEG_GRID, SEG_GRID), jnp.int32),
            pltpu.VMEM((4, 2, ROWS, WIDE), bf16),
            pltpu.VMEM((4, 2, ROWS, WIDE), bf16),
            dma((6,)),
            dma((4, 2)),
            dma((4,)),
        ],
        compiler_params=pltpu.CompilerParams(vmem_limit_bytes=64 * 1024 * 1024),
    )(screens, chosen, row_shift, column_shift, fractions, pistons, segment_map)
    return pl.pallas_call(
        kernel,
        out_shape=jax.ShapeDtypeStruct((ROWS, SHARE), f32),
        in_specs=[hbm, vmem, vmem, hbm],
        out_specs=vmem,
        scratch_shapes=[
            pltpu.VMEM((ROWS, SHARE), bf16),
            pltpu.VMEM((2, 2, ROWS, WIDE), bf16),
            pltpu.VMEM((2, 2, ROWS, WIDE), bf16),
            pltpu.VMEM((8, 128), f32),
            pltpu.VMEM((1024, CHUNK), bf16),
            pltpu.VMEM((256 * PIECES, 1024), bf16),
            pltpu.VMEM((256 * PIECES, CHUNK), f32),
            pltpu.VMEM((CHUNKS, ROWS, CHUNK), f32),
            pltpu.VMEM((2, CHUNKS, ROWS, CHUNK), LINK),
            pltpu.VMEM((2, CHUNKS, ROWS, CHUNK), LINK),
            pltpu.VMEM((CHUNKS, ROWS, CHUNK), LINK),
            pltpu.VMEM((CHUNKS, ROWS, CHUNK), LINK),
            pltpu.VMEM((HALF, ROWS, CHUNK), LINK),
            pltpu.VMEM((HALF, ROWS, CHUNK), LINK),
            pltpu.VMEM((HALF, ROWS, CHUNK), f32),
            pltpu.VMEM((2, CHUNKS, ROWS, CHUNK), f32),
            pltpu.VMEM((CHUNKS, ROWS, CHUNK), f32),
            pltpu.VMEM((CHUNKS, ROWS, CHUNK), f32),
            pltpu.VMEM((4, ROWS, CHUNK), f32),
            pltpu.VMEM((8, SHARE), f32),
            pltpu.VMEM((10, 8, 128), f32),
            pltpu.VMEM((3, 8, 128), f32),
            pltpu.VMEM((3, 16, 8, 128), f32),
            dma((3,)),
            dma((2,)),
            dma((2,)),
            dma((2,)),
            dma((2, CHUNKS)),
            dma((2, CHUNKS)),
            dma((CHUNKS,)),
            dma((CHUNKS,)),
            dma((HALF,)),
            dma((HALF,)),
            dma((2, 3, 16)),
        ],
        compiler_params=pltpu.CompilerParams(
            collective_id=0, has_side_effects=True, vmem_limit_bytes=64 * 1024 * 1024
        ),
    )(placed, prm, steps, amplitude)


def solution(mesh):
    return jax.shard_map(
        body,
        mesh=mesh,
        in_specs=(
            P("layer", "tile", None),
            P("layer"),
            P("layer"),
            P("layer"),
            P("layer", None),
            P(),
            P(),
            P("tile", None),
        ),
        out_specs=P("tile", "layer"),
        check_vma=False,
    )
```

```python
import functools
import math

import jax
import jax.numpy as jnp
from jax import lax
from jax.experimental import pallas as pl
from jax.experimental.pallas import tpu as pltpu
from jax.sharding import PartitionSpec as P

PUPIL = 8192
PADDED = 16384
SEG_GRID = 32
DOT_RADIUS = 2
ROWS = 128
SHARE = 2048
CHUNK = 256
CHUNKS = SHARE // CHUNK
WIDE = SHARE + 128
PIECES = 2
HALF = CHUNKS // 2
LINK = jnp.bfloat16
SPAN = 500.0
phase_step = math.pi / 2
f32 = jnp.float32
bf16 = jnp.bfloat16
MESH = pl.DeviceIdType.MESH


def nearest(x):
    return jnp.floor(x + 0.5)


def turn_sincos(u):
    r = u - nearest(u)
    q = nearest(4.0 * r)
    x = (r - 0.25 * q) * (2.0 * math.pi)
    z = x * x
    s = x * (1.0 + z * (-1.0 / 6 + z * (1.0 / 120 + z * (-1.0 / 5040 + z * (1.0 / 362880)))))
    c = 1.0 + z * (-0.5 + z * (1.0 / 24 + z * (-1.0 / 720 + z * (1.0 / 40320))))
    odd = jnp.abs(q) == 1.0
    cos = jnp.where(odd, s, c)
    sin = jnp.where(odd, c, s)
    cos = jnp.where((q == 1.0) | (jnp.abs(q) == 2.0), -cos, cos)
    sin = jnp.where((q == -1.0) | (jnp.abs(q) == 2.0), -sin, sin)
    return cos, sin


def to_link(u):
    r = u - nearest(u)
    v = jnp.exp2(jnp.abs(r) * SPAN - 0.25 * SPAN)
    return jnp.where(r < 0.0, -v, v).astype(LINK)


def from_link(v):
    v = v.astype(f32)
    r = jnp.log(jnp.abs(v)) * (1.0 / (math.log(2.0) * SPAN)) + 0.25
    return jnp.where(v < 0.0, -r, r)


def place_kernel(
    screens, chosen_hbm, row_shift_hbm, column_shift_hbm, fractions_hbm, pistons_hbm, map_hbm,
    aligned, facts,
    chosen, column_shift, row_shift, fractions, pistons, segment_map,
    raw, ready, small_sem, load_sem, store_sem,
):
    small = [
        pltpu.make_async_copy(source, target, small_sem.at[i])
        for i, (source, target) in enumerate(
            (
                (chosen_hbm, chosen),
                (column_shift_hbm, column_shift),
                (row_shift_hbm, row_shift),
                (fractions_hbm, fractions),
                (pistons_hbm, pistons),
                (map_hbm, segment_map),
            )
        )
    ]
    for copy in small:
        copy.start()
    layer = lax.axis_index("layer")
    tile = lax.axis_index("tile")
    sibling = (layer // 2) * 2 + 1 - layer % 2
    order = ((sibling + 2) % 4, (layer + 2) % 4, sibling, layer)

    def load(area, e):
        start = (column_shift[e] // 128 + 16 * area) * 128
        return pltpu.make_async_copy(
            screens.at[chosen[e], :, pl.ds(pl.multiple_of(start, 128), WIDE)],
            raw.at[area, e],
            load_sem.at[area, e],
        )

    def store(area):
        return pltpu.make_async_copy(ready.at[area], aligned.at[area], store_sem.at[area])

    for copy in small[:2]:
        copy.wait()
    for area in order:
        for e in range(2):
            load(area, e).start()
    for copy in small[2:]:
        copy.wait()
    for e in range(2):
        facts[pl.ds(4 * e, 1), :] = jnp.full((1, 128), row_shift[e], jnp.int32).astype(f32)
        facts[pl.ds(4 * e + 1, 1), :] = jnp.full((1, 128), fractions[e, 0], f32)
        facts[pl.ds(4 * e + 2, 1), :] = jnp.full((1, 128), fractions[e, 1], f32)
        facts[pl.ds(4 * e + 3, 1), :] = jnp.zeros((1, 128), f32)
    for k in range(CHUNKS):
        piston = pistons[segment_map[tile // 2, layer * CHUNKS + k]]
        facts[pl.ds(8 + k, 1), :] = jnp.full((1, 128), piston * (0.5 / math.pi), f32)
    lane = lax.broadcasted_iota(jnp.int32, (ROWS, 128), 1)
    for area in order:
        for e in range(2):
            load(area, e).wait()
            part = column_shift[e] % 128
            keep = lane < 128 - part

            def rolled(j):
                block = raw[area, e, :, pl.ds(128 * j, 128)].astype(f32)
                return pltpu.roll(block, (128 - part) % 128, 1)

            previous = rolled(0)
            for j in range(16):
                following = rolled(j + 1)
                ready[area, e, :, pl.ds(128 * j, 128)] = jnp.where(
                    keep, previous, following
                ).astype(bf16)
                previous = following
            ready[area, e, :, pl.ds(SHARE, 128)] = previous.astype(bf16)
        store(area).start()
    for area in order:
        store(area).wait()


def kernel(
    placed, facts, amplitude, out,
    amp, aligned, shared, sib_prm, taps, weights, product, own,
    x_out, x_in, z_out, z_in, p_out, p_in, held, lows,
    field_re, field_im, rows_t, cols_t, acc, message, arrived,
    load_sem, share_send, share_recv, prm_sem, x_send, x_recv, z_send, z_recv,
    p_send, p_recv, sum_sem,
):
    layer = lax.axis_index("layer")
    tile = lax.axis_index("tile")
    pair, core = layer // 2, layer % 2
    sibling = pair * 2 + 1 - core
    partner = (1 - pair) * 2 + core
    crossed = (1 - pair) * 2 + 1 - core
    before = (tile + 63) % 64
    after = (tile + 1) % 64

    flip = (tile % 32 == 0).astype(jnp.int32)
    target = jnp.where(tile % 32 == 0, partner, layer)
    origin = jnp.where(tile % 32 == 31, partner, layer)
    x = (tile // 32) * 2 + pair
    y = (tile // 8) % 4
    z = tile % 8

    def at(x, y, z, core):
        return (x % 2) * 2 + core, (x // 2) * 32 + y * 8 + z

    def z_peer(d):
        return at(x, y, (z + d) % 8, core)

    def y_peer(d):
        place = (y * 2 + core + d) % 8
        return at(x, place // 2, z, place % 2)

    def x_peer(d):
        return at((x + d) % 4, y, z, core)

    def near_peer(d):
        place = (z * 2 + core + d) % 16
        return at(x, y, place // 2, place % 2)

    def far_peer(d):
        place = (y * 4 + x + d) % 16
        return at(place % 4, place // 4, z, core)

    def ring(step, size):
        return min(step, size - step)

    def near_far(d):
        return -ring(d // 2, 8)

    def far_far(d):
        return -ring(d % 4, 4) - ring(d // 4, 4)

    stages = (
        (16, near_peer, sorted(range(1, 16), key=near_far)),
        (16, far_peer, sorted(range(1, 16), key=far_far)),
    )

    loads = [
        pltpu.make_async_copy(placed.at[area], aligned.at[slot], load_sem.at[slot])
        for slot, area in enumerate((partner, layer))
    ]
    loads.append(
        pltpu.make_async_copy(
            amplitude.at[:, pl.ds(pl.multiple_of(layer * SHARE, SHARE), SHARE)],
            amp,
            load_sem.at[2],
        )
    )
    for load in loads:
        load.start()

    barrier = pltpu.get_barrier_semaphore()
    greeted = [(sibling, tile), (target, before), (origin, after)]
    greeted += [peer(d) for _, peer, order in stages for d in order]
    for device in greeted:
        pl.semaphore_signal(barrier, inc=1, device_id=device, device_id_type=MESH)

    pl.semaphore_wait(barrier, len(greeted))
    send_prm = pltpu.make_async_remote_copy(
        src_ref=facts.at[pl.ds(0, 8), :], dst_ref=sib_prm, send_sem=prm_sem.at[0], recv_sem=prm_sem.at[1],
        device_id=(sibling, tile), device_id_type=MESH,
    )
    send_prm.start()
    def share(piece):
        area, slot = (crossed, 0) if piece % 2 == 0 else (sibling, 1)
        cols = pl.ds(1024, WIDE - 1024) if piece < 2 else pl.ds(0, 1024)
        return pltpu.make_async_remote_copy(
            src_ref=placed.at[area, :, :, cols], dst_ref=shared.at[slot, :, :, cols],
            send_sem=share_send.at[piece], recv_sem=share_recv.at[piece],
            device_id=(sibling, tile), device_id_type=MESH,
        )

    for piece in range(4):
        share(piece).start()

    row_id = lax.broadcasted_iota(jnp.int32, (ROWS, 128), 0) + tile * ROWS
    for k in (1, 2):
        cos, sin = turn_sincos((row_id * k).astype(f32) * (1.0 / PADDED))
        for half in range(2):
            rows_t[2 * k - 2, :, pl.ds(128 * half, 128)] = cos
            rows_t[2 * k - 1, :, pl.ds(128 * half, 128)] = sin
    kind = lax.broadcasted_iota(jnp.int32, (8, SHARE), 0)
    col_id = lax.broadcasted_iota(jnp.int32, (8, SHARE), 1) + layer * SHARE
    cos, sin = turn_sincos((col_id * ((kind + 1) // 2)).astype(f32) * (1.0 / PADDED))
    table = jnp.where((kind == 2) | (kind == 4), sin, cos)
    cols_t[...] = jnp.where(kind < 5, table, 0.0)
    acc[...] = jnp.zeros_like(acc)

    gap = (
        lax.broadcasted_iota(jnp.int32, (256, 128), 1)
        - lax.broadcasted_iota(jnp.int32, (256, 128), 0)
        + 128
    ).astype(f32)
    for source in range(2):
        table = facts if source == 0 else sib_prm
        if source == 1:
            send_prm.wait()
        for e in range(2):
            shift = table[pl.ds(4 * e, 1), :]
            frac_row = table[pl.ds(4 * e + 1, 1), :]
            frac_col = table[pl.ds(4 * e + 2, 1), :]
            down = jnp.where(gap == shift, 1.0 - frac_row, 0.0) + jnp.where(
                gap == shift + 1.0, frac_row, 0.0
            )
            for tap in range(2):
                left = down * ((frac_col if tap else 1.0 - frac_col) * (0.5 / math.pi))
                place = (source * 2 + e) * 256 + tap * 128
                for piece in range(PIECES):
                    part = left.astype(bf16)
                    weights[pl.ds(256 * piece, 256), pl.ds(place, 128)] = part
                    left = left - part.astype(f32)

    def fill(slot, k):
        for source in range(2):
            for e in range(2):
                cols = pl.ds(pl.multiple_of(k * CHUNK, CHUNK), CHUNK + 128)
                block = aligned[slot, e, :, cols] if source == 0 else shared[slot, e, :, cols]
                place = (source * 2 + e) * 256
                taps[pl.ds(place, 128), :] = block[:, :CHUNK]
                moved = pltpu.roll(block, CHUNK + 127, 1)
                taps[pl.ds(place + 128, 128), :] = moved[:, :CHUNK]
        product[...] = jnp.dot(weights[...], taps[...], preferred_element_type=f32)

    def summed(first_row, rows):
        total = product[pl.ds(first_row, rows), :]
        for piece in range(1, PIECES):
            total = total + product[pl.ds(256 * piece + first_row, rows), :]
        return total

    def across(half, k):
        return pltpu.make_async_remote_copy(
            src_ref=x_out.at[half, k], dst_ref=x_in.at[half, k],
            send_sem=x_send.at[half, k], recv_sem=x_recv.at[half, k],
            device_id=(partner, tile), device_id_type=MESH,
        )

    def upward(k):
        return pltpu.make_async_remote_copy(
            src_ref=z_out.at[k], dst_ref=z_in.at[k],
            send_sem=z_send.at[k], recv_sem=z_recv.at[k],
            device_id=(target, before), device_id_type=MESH,
        )

    def upward_first(k):
        return pltpu.make_async_remote_copy(
            src_ref=p_out.at[k], dst_ref=p_in.at[k],
            send_sem=p_send.at[k], recv_sem=p_recv.at[k],
            device_id=(target, before), device_id_type=MESH,
        )

    quarters = [pl.ds(32 * block, 32) for block in range(4)]

    def relay(i):
        upward_first(i).wait_recv()
        for rows in quarters:
            x_out[1, i, rows, :] = to_link(held[i, rows, :] + from_link(p_in[i, rows, :]))
        across(1, i).start()
        k = i + HALF
        across(0, k).wait_recv()
        for rows in quarters:
            z_out[k, rows, :] = to_link(
                lows[1 - flip, k, rows, :] + from_link(x_in[0, k, rows, :])
            )
        upward(k).start()

    loads[0].wait()
    loads[1].wait()
    share(0).wait_recv()

    @pl.loop(0, HALF)
    def _(i):
        k = i + HALF
        def awaited(piece):
            @pl.when(i == 0)
            def _():
                share(piece).wait_recv()

        def sums(slot, k, target, index, convert):
            fill(slot, k)
            for block, rows in enumerate(quarters):
                target[(*index, rows, slice(None))] = convert(summed(128 + 32 * block, 32))
                lows[slot, k, rows, :] = summed(32 * block, 32)

        sums(0, k, x_out, (1, k), to_link)
        across(1, k).start()
        awaited(1)
        sums(1, k, own, (k,), lambda v: v)
        for rows in quarters:
            x_out[0, k, rows, :] = to_link(lows[flip, k, rows, :])
        across(0, k).start()
        awaited(2)
        sums(0, i, held, (i,), lambda v: v)
        awaited(3)
        sums(1, i, own, (i,), lambda v: v)
        for rows in quarters:
            p_out[i, rows, :] = to_link(lows[flip, i, rows, :])
        upward_first(i).start()
        for rows in quarters:
            z_out[i, rows, :] = to_link(lows[1 - flip, i, rows, :])
        upward(i).start()

        @pl.when(i >= 1)
        def _():
            relay(i - 1)

    relay(HALF - 1)
    loads[2].wait()

    @pl.loop(0, CHUNKS)
    def _(i):
        k = i // 2 + HALF * (1 - i % 2)
        across(1, k).wait_recv()
        upward(k).wait_recv()
        line = facts[pl.ds(8 + k, 1), :]
        piston = jnp.concatenate([line, line], axis=1)
        sums = [jnp.zeros((8, CHUNK), f32) for _ in range(10)]
        cols = pl.ds(pl.multiple_of(k * CHUNK, CHUNK), CHUNK)
        for block in range(8):
            rows = pl.ds(16 * block, 16)
            turns = (
                own[k, rows, :]
                + from_link(x_in[1, k, rows, :])
                + from_link(z_in[k, rows, :])
                + piston
            )
            cos, sin = turn_sincos(turns)
            size = amp[rows, cols].astype(f32)
            real, imag = size * cos, size * sin
            field_re[k, rows, :] = real
            field_im[k, rows, :] = imag
            for base, part in ((0, real), (5, imag)):
                sums[base] = sums[base] + (part[:8] + part[8:])
                for j in range(4):
                    wide = part * rows_t[j, rows, :]
                    sums[base + 1 + j] = sums[base + 1 + j] + (wide[:8] + wide[8:])
        for j in range(10):
            line = jnp.sum(sums[j], axis=0, keepdims=True)
            spread = line * cols_t[:, cols]
            acc[j] = acc[j] + (spread[:, :128] + spread[:, 128:])

    spot = lax.broadcasted_iota(jnp.int32, (8, 128), 1)
    packed = jnp.zeros((8, 128), f32)
    for j in range(10):
        packed = jnp.where(spot == j, jnp.sum(acc[j], axis=1, keepdims=True), packed)
    line_id = lax.broadcasted_iota(jnp.int32, (8, 128), 0)
    total = jnp.where(line_id == 0, packed, 0.0)
    for k in range(1, 5):
        total = total + jnp.where(line_id == k, pltpu.roll(packed, 128 - 16 * k, 1), 0.0)
    total = jnp.sum(total, axis=0, keepdims=True)
    sent = []
    for stage, (size, peer, order) in enumerate(stages):
        message[stage, pl.ds(0, 1), :] = total
        copies = [
            pltpu.make_async_remote_copy(
                src_ref=message.at[stage, pl.ds(0, 1), :],
                dst_ref=arrived.at[stage, pl.ds(d, 1), :],
                send_sem=sum_sem.at[0, stage, d], recv_sem=sum_sem.at[1, stage, d],
                device_id=peer(d), device_id_type=MESH,
            )
            for d in order
        ]
        for copy in copies:
            copy.start()
        for copy in copies:
            copy.wait_recv()
        arrived[stage, pl.ds(0, 1), :] = total
        total = jnp.sum(arrived[stage], axis=0, keepdims=True)
        sent += copies
    total = pltpu.roll(jnp.broadcast_to(total, (8, 128)), 0, 1, stride=16, stride_axis=0)

    row_kind = spot % 5
    col_kind = lax.broadcasted_iota(jnp.int32, (8, 128), 0)
    row_freq = (row_kind + 1) // 2
    col_freq = (col_kind + 1) // 2
    inside = (row_freq * row_freq + col_freq * col_freq <= DOT_RADIUS**2) & (spot < 10)
    factor = (
        jnp.where(inside, 1.0 / (PADDED * PADDED), 0.0)
        * jnp.where(row_kind > 0, 2.0, 1.0)
        * jnp.where(col_kind > 0, 2.0, 1.0)
    )
    turned = jnp.where(spot < 5, -pltpu.roll(total, 123, 1), pltpu.roll(total, 5, 1))
    mix = factor * ((math.cos(phase_step) - 1.0) * total + math.sin(phase_step) * turned)
    for k in range(CHUNKS):
        cols = pl.ds(CHUNK * k, CHUNK)
        lines = [
            jnp.sum(mix[:, j : j + 1] * cols_t[:, cols], axis=0, keepdims=True) for j in range(10)
        ]
        for block in range(8):
            rows = pl.ds(16 * block, 16)
            real = field_re[k, rows, :] + lines[0]
            imag = field_im[k, rows, :] + lines[5]
            for j in range(4):
                table = rows_t[j, rows, :]
                real = real + table * lines[1 + j]
                imag = imag + table * lines[6 + j]
            out[rows, cols] = real * real + imag * imag

    for piece in range(4):
        share(piece).wait_send()
    for copy in sent:
        copy.wait_send()
    for k in range(CHUNKS):
        upward(k).wait_send()
        across(1, k).wait_send()
    for k in range(HALF):
        upward_first(k).wait_send()
        across(0, k + HALF).wait_send()


def body(screens, chosen, row_shift, column_shift, fractions, pistons, segment_map, amplitude):
    hbm = pl.BlockSpec(memory_space=pltpu.HBM)
    vmem = pl.BlockSpec(memory_space=pltpu.VMEM)
    dma = pltpu.SemaphoreType.DMA
    placed, facts = pl.pallas_call(
        place_kernel,
        out_shape=(
            jax.ShapeDtypeStruct((4, 2, ROWS, WIDE), bf16),
            jax.ShapeDtypeStruct((16, 128), f32),
        ),
        in_specs=[hbm] * 7,
        out_specs=(hbm, vmem),
        scratch_shapes=[
            pltpu.SMEM((2,), jnp.int32),
            pltpu.SMEM((2,), jnp.int32),
            pltpu.SMEM((2,), jnp.int32),
            pltpu.SMEM((2, 2), f32),
            pltpu.SMEM(pistons.shape, f32),
            pltpu.SMEM((SEG_GRID, SEG_GRID), jnp.int32),
            pltpu.VMEM((4, 2, ROWS, WIDE), bf16),
            pltpu.VMEM((4, 2, ROWS, WIDE), bf16),
            dma((6,)),
            dma((4, 2)),
            dma((4,)),
        ],
        compiler_params=pltpu.CompilerParams(vmem_limit_bytes=64 * 1024 * 1024),
    )(screens, chosen, row_shift, column_shift, fractions, pistons, segment_map)
    return pl.pallas_call(
        kernel,
        out_shape=jax.ShapeDtypeStruct((ROWS, SHARE), f32),
        in_specs=[hbm, vmem, hbm],
        out_specs=vmem,
        scratch_shapes=[
            pltpu.VMEM((ROWS, SHARE), bf16),
            pltpu.VMEM((2, 2, ROWS, WIDE), bf16),
            pltpu.VMEM((2, 2, ROWS, WIDE), bf16),
            pltpu.VMEM((8, 128), f32),
            pltpu.VMEM((1024, CHUNK), bf16),
            pltpu.VMEM((256 * PIECES, 1024), bf16),
            pltpu.VMEM((256 * PIECES, CHUNK), f32),
            pltpu.VMEM((CHUNKS, ROWS, CHUNK), f32),
            pltpu.VMEM((2, CHUNKS, ROWS, CHUNK), LINK),
            pltpu.VMEM((2, CHUNKS, ROWS, CHUNK), LINK),
            pltpu.VMEM((CHUNKS, ROWS, CHUNK), LINK),
            pltpu.VMEM((CHUNKS, ROWS, CHUNK), LINK),
            pltpu.VMEM((HALF, ROWS, CHUNK), LINK),
            pltpu.VMEM((HALF, ROWS, CHUNK), LINK),
            pltpu.VMEM((HALF, ROWS, CHUNK), f32),
            pltpu.VMEM((2, CHUNKS, ROWS, CHUNK), f32),
            pltpu.VMEM((CHUNKS, ROWS, CHUNK), f32),
            pltpu.VMEM((CHUNKS, ROWS, CHUNK), f32),
            pltpu.VMEM((4, ROWS, CHUNK), f32),
            pltpu.VMEM((8, SHARE), f32),
            pltpu.VMEM((10, 8, 128), f32),
            pltpu.VMEM((2, 8, 128), f32),
            pltpu.VMEM((2, 16, 128), f32),
            dma((3,)),
            dma((4,)),
            dma((4,)),
            dma((2,)),
            dma((2, CHUNKS)),
            dma((2, CHUNKS)),
            dma((CHUNKS,)),
            dma((CHUNKS,)),
            dma((HALF,)),
            dma((HALF,)),
            dma((2, 2, 16)),
        ],
        compiler_params=pltpu.CompilerParams(
            collective_id=0, has_side_effects=True, vmem_limit_bytes=52 * 1024 * 1024
        ),
    )(placed, facts, amplitude)


def solution(mesh):
    return jax.shard_map(
        body,
        mesh=mesh,
        in_specs=(
            P("layer", "tile", None),
            P("layer"),
            P("layer"),
            P("layer"),
            P("layer", None),
            P(),
            P(),
            P("tile", None),
        ),
        out_specs=P("tile", "layer"),
        check_vma=False,
    )
```

```python
import functools
import math

import jax
import jax.numpy as jnp
from jax import lax
from jax.experimental import pallas as pl
from jax.experimental.pallas import tpu as pltpu
from jax.sharding import PartitionSpec as P

PUPIL = 8192
PADDED = 16384
SEG_GRID = 32
DOT_RADIUS = 2
ROWS = 128
SHARE = 2048
CHUNK = 256
CHUNKS = SHARE // CHUNK
WIDE = SHARE + 128
PIECES = 2
HALF = CHUNKS // 2
LINK = jnp.bfloat16
SPAN = 500.0
phase_step = math.pi / 2
f32 = jnp.float32
bf16 = jnp.bfloat16
MESH = pl.DeviceIdType.MESH


def nearest(x):
    return jnp.floor(x + 0.5)


def turn_sincos(u):
    r = u - nearest(u)
    q = nearest(4.0 * r)
    x = (r - 0.25 * q) * (2.0 * math.pi)
    z = x * x
    s = x * (1.0 + z * (-1.0 / 6 + z * (1.0 / 120 + z * (-1.0 / 5040 + z * (1.0 / 362880)))))
    c = 1.0 + z * (-0.5 + z * (1.0 / 24 + z * (-1.0 / 720 + z * (1.0 / 40320))))
    odd = jnp.abs(q) == 1.0
    cos = jnp.where(odd, s, c)
    sin = jnp.where(odd, c, s)
    cos = jnp.where((q == 1.0) | (jnp.abs(q) == 2.0), -cos, cos)
    sin = jnp.where((q == -1.0) | (jnp.abs(q) == 2.0), -sin, sin)
    return cos, sin


def to_link(u):
    r = u - nearest(u)
    v = jnp.exp2(jnp.abs(r) * SPAN - 0.25 * SPAN)
    return jnp.where(r < 0.0, -v, v).astype(LINK)


def from_link(v):
    v = v.astype(f32)
    r = jnp.log(jnp.abs(v)) * (1.0 / (math.log(2.0) * SPAN)) + 0.25
    return jnp.where(v < 0.0, -r, r)


def place_kernel(
    screens, chosen_hbm, row_shift_hbm, column_shift_hbm, fractions_hbm, pistons_hbm, map_hbm,
    aligned, facts_hbm,
    facts, chosen, column_shift, row_shift, fractions, pistons, segment_map,
    raw, ready, small_sem, load_sem, store_sem,
):
    small = [
        pltpu.make_async_copy(source, target, small_sem.at[i])
        for i, (source, target) in enumerate(
            (
                (chosen_hbm, chosen),
                (column_shift_hbm, column_shift),
                (row_shift_hbm, row_shift),
                (fractions_hbm, fractions),
                (pistons_hbm, pistons),
                (map_hbm, segment_map),
            )
        )
    ]
    for copy in small:
        copy.start()
    layer = lax.axis_index("layer")
    tile = lax.axis_index("tile")
    sibling = (layer // 2) * 2 + 1 - layer % 2
    order = ((sibling + 2) % 4, (layer + 2) % 4, sibling, layer)

    def load(area, e):
        start = (column_shift[e] // 128 + 16 * area) * 128
        return pltpu.make_async_copy(
            screens.at[chosen[e], :, pl.ds(pl.multiple_of(start, 128), WIDE)],
            raw.at[area, e],
            load_sem.at[area, e],
        )

    def store(area):
        return pltpu.make_async_copy(ready.at[area], aligned.at[area], store_sem.at[area])

    for copy in small[:2]:
        copy.wait()
    for area in order:
        for e in range(2):
            load(area, e).start()
    for copy in small[2:]:
        copy.wait()
    for e in range(2):
        facts[pl.ds(4 * e, 1), :] = jnp.full((1, 128), row_shift[e], jnp.int32).astype(f32)
        facts[pl.ds(4 * e + 1, 1), :] = jnp.full((1, 128), fractions[e, 0], f32)
        facts[pl.ds(4 * e + 2, 1), :] = jnp.full((1, 128), fractions[e, 1], f32)
        facts[pl.ds(4 * e + 3, 1), :] = jnp.zeros((1, 128), f32)
    for k in range(CHUNKS):
        piston = pistons[segment_map[tile // 2, layer * CHUNKS + k]]
        facts[pl.ds(8 + k, 1), :] = jnp.full((1, 128), piston * (0.5 / math.pi), f32)
    keep_facts = pltpu.make_async_copy(facts, facts_hbm.at[pl.ds(0, 16), :], small_sem.at[6])
    keep_facts.start()
    lane = lax.broadcasted_iota(jnp.int32, (ROWS, 128), 1)
    for area in order:
        for e in range(2):
            load(area, e).wait()
            part = column_shift[e] % 128
            keep = lane < 128 - part

            def rolled(j):
                block = raw[area, e, :, pl.ds(128 * j, 128)]
                return pltpu.roll(block, (128 - part) % 128, 1)

            previous = rolled(0)
            for j in range(16):
                following = rolled(j + 1)
                ready[area, e, :, pl.ds(128 * j, 128)] = jnp.where(keep, previous, following)
                previous = following
            ready[area, e, :, pl.ds(SHARE, 128)] = previous
        store(area).start()
    for area in order:
        store(area).wait()
    keep_facts.wait()


def kernel(
    placed, facts_hbm, amplitude, out,
    facts, amp, aligned, shared, sib_prm, taps, weights, product, own,
    x_out, x_in, z_out, z_in, p_out, p_in, held, lows,
    field_re, field_im, rows_t, cols_t, acc, message, arrived,
    load_sem, share_send, share_recv, prm_sem, x_send, x_recv, z_send, z_recv,
    p_send, p_recv, sum_sem,
):
    layer = lax.axis_index("layer")
    tile = lax.axis_index("tile")
    pair, core = layer // 2, layer % 2
    sibling = pair * 2 + 1 - core
    partner = (1 - pair) * 2 + core
    crossed = (1 - pair) * 2 + 1 - core
    before = (tile + 63) % 64
    after = (tile + 1) % 64

    flip = (tile % 32 == 0).astype(jnp.int32)
    target = jnp.where(tile % 32 == 0, partner, layer)
    origin = jnp.where(tile % 32 == 31, partner, layer)
    x = (tile // 32) * 2 + pair
    y = (tile // 8) % 4
    z = tile % 8

    def at(x, y, z, core):
        return (x % 2) * 2 + core, (x // 2) * 32 + y * 8 + z

    def z_peer(d):
        return at(x, y, (z + d) % 8, core)

    def y_peer(d):
        place = (y * 2 + core + d) % 8
        return at(x, place // 2, z, place % 2)

    def x_peer(d):
        return at((x + d) % 4, y, z, core)

    def near_peer(d):
        place = (z * 2 + core + d) % 16
        return at(x, y, place // 2, place % 2)

    def far_peer(d):
        place = (y * 4 + x + d) % 16
        return at(place % 4, place // 4, z, core)

    def ring(step, size):
        return min(step, size - step)

    def near_far(d):
        return -ring(d // 2, 8)

    def far_far(d):
        return -ring(d % 4, 4) - ring(d // 4, 4)

    stages = (
        (16, near_peer, sorted(range(1, 16), key=near_far)),
        (16, far_peer, sorted(range(1, 16), key=far_far)),
    )

    loads = [
        pltpu.make_async_copy(placed.at[area], aligned.at[slot], load_sem.at[slot])
        for slot, area in enumerate((partner, layer))
    ]
    loads.append(
        pltpu.make_async_copy(
            amplitude.at[:, pl.ds(pl.multiple_of(layer * SHARE, SHARE), SHARE)],
            amp,
            load_sem.at[2],
        )
    )
    loads.append(
        pltpu.make_async_copy(facts_hbm.at[pl.ds(0, 16), :], facts, load_sem.at[3])
    )
    for load in loads:
        load.start()

    barrier = pltpu.get_barrier_semaphore()
    greeted = [(sibling, tile), (target, before), (origin, after)]
    greeted += [peer(d) for _, peer, order in stages for d in order]
    for device in greeted:
        pl.semaphore_signal(barrier, inc=1, device_id=device, device_id_type=MESH)

    pl.semaphore_wait(barrier, len(greeted))
    send_prm = pltpu.make_async_remote_copy(
        src_ref=facts.at[pl.ds(0, 8), :], dst_ref=sib_prm, send_sem=prm_sem.at[0], recv_sem=prm_sem.at[1],
        device_id=(sibling, tile), device_id_type=MESH,
    )
    loads[3].wait()
    send_prm.start()
    first, second = (0, 384), (1024, 384)
    rest_first, rest_second = (384, 640), (1408, WIDE - 1408)
    pieces = [(0, second), (0, first), (1, first), (1, second)]
    pieces += [(0, rest_second), (0, rest_first), (1, rest_first), (1, rest_second)]

    def share(piece):
        slot, (start, width) = pieces[piece]
        area = sibling if slot else crossed
        cols = pl.ds(start, width)
        return pltpu.make_async_remote_copy(
            src_ref=placed.at[area, :, :, cols], dst_ref=shared.at[slot, :, :, cols],
            send_sem=share_send.at[piece], recv_sem=share_recv.at[piece],
            device_id=(sibling, tile), device_id_type=MESH,
        )

    for piece in range(8):
        share(piece).start()

    gap = (
        lax.broadcasted_iota(jnp.int32, (256, 128), 1)
        - lax.broadcasted_iota(jnp.int32, (256, 128), 0)
        + 128
    ).astype(f32)
    for source in range(2):
        table = facts if source == 0 else sib_prm
        if source == 1:
            send_prm.wait()
        for e in range(2):
            shift = table[pl.ds(4 * e, 1), :]
            frac_row = table[pl.ds(4 * e + 1, 1), :]
            frac_col = table[pl.ds(4 * e + 2, 1), :]
            down = jnp.where(gap == shift, 1.0 - frac_row, 0.0) + jnp.where(
                gap == shift + 1.0, frac_row, 0.0
            )
            for tap in range(2):
                left = down * ((frac_col if tap else 1.0 - frac_col) * (0.5 / math.pi))
                place = (source * 2 + e) * 256 + tap * 128
                for piece in range(PIECES):
                    part = left.astype(bf16)
                    weights[pl.ds(256 * piece, 256), pl.ds(place, 128)] = part
                    left = left - part.astype(f32)

    def fill(slot, k):
        for source in range(2):
            for e in range(2):
                cols = pl.ds(pl.multiple_of(k * CHUNK, CHUNK), CHUNK + 128)
                block = aligned[slot, e, :, cols] if source == 0 else shared[slot, e, :, cols]
                place = (source * 2 + e) * 256
                taps[pl.ds(place, 128), :] = block[:, :CHUNK]
                moved = pltpu.roll(block, CHUNK + 127, 1)
                taps[pl.ds(place + 128, 128), :] = moved[:, :CHUNK]
        product[...] = jnp.dot(weights[...], taps[...], preferred_element_type=f32)

    def summed(first_row, rows):
        total = product[pl.ds(first_row, rows), :]
        for piece in range(1, PIECES):
            total = total + product[pl.ds(256 * piece + first_row, rows), :]
        return total

    def across(half, k):
        return pltpu.make_async_remote_copy(
            src_ref=x_out.at[half, k], dst_ref=x_in.at[half, k],
            send_sem=x_send.at[half, k], recv_sem=x_recv.at[half, k],
            device_id=(partner, tile), device_id_type=MESH,
        )

    def upward(k):
        return pltpu.make_async_remote_copy(
            src_ref=z_out.at[k], dst_ref=z_in.at[k],
            send_sem=z_send.at[k], recv_sem=z_recv.at[k],
            device_id=(target, before), device_id_type=MESH,
        )

    def upward_first(k):
        return pltpu.make_async_remote_copy(
            src_ref=p_out.at[k], dst_ref=p_in.at[k],
            send_sem=p_send.at[k], recv_sem=p_recv.at[k],
            device_id=(target, before), device_id_type=MESH,
        )

    quarters = [pl.ds(32 * block, 32) for block in range(4)]

    def relay(i):
        upward_first(i).wait_recv()
        for rows in quarters:
            x_out[1, i, rows, :] = to_link(held[i, rows, :] + from_link(p_in[i, rows, :]))
        across(1, i).start()
        k = i + HALF
        across(0, k).wait_recv()
        for rows in quarters:
            z_out[k, rows, :] = to_link(
                lows[1 - flip, k, rows, :] + from_link(x_in[0, k, rows, :])
            )
        upward(k).start()

    loads[0].wait()
    loads[1].wait()

    @pl.loop(0, HALF)
    def _(i):
        k = i + HALF
        def awaited(piece):
            @pl.when(i == 0)
            def _():
                share(piece).wait_recv()

            @pl.when(i == 1)
            def _():
                share(piece + 4).wait_recv()

        def sums(slot, k, target, index, convert):
            fill(slot, k)
            for block, rows in enumerate(quarters):
                target[(*index, rows, slice(None))] = convert(summed(128 + 32 * block, 32))
                lows[slot, k, rows, :] = summed(32 * block, 32)

        awaited(0)
        sums(0, k, x_out, (1, k), to_link)
        across(1, k).start()
        awaited(1)
        sums(0, i, held, (i,), lambda v: v)
        awaited(2)
        sums(1, i, own, (i,), lambda v: v)
        for rows in quarters:
            p_out[i, rows, :] = to_link(lows[flip, i, rows, :])
        upward_first(i).start()
        for rows in quarters:
            z_out[i, rows, :] = to_link(lows[1 - flip, i, rows, :])
        upward(i).start()
        awaited(3)
        sums(1, k, own, (k,), lambda v: v)
        for rows in quarters:
            x_out[0, k, rows, :] = to_link(lows[flip, k, rows, :])
        across(0, k).start()

        @pl.when(i >= 1)
        def _():
            relay(i - 1)

    relay(HALF - 1)

    row_id = lax.broadcasted_iota(jnp.int32, (ROWS, 128), 0) + tile * ROWS
    for k in (1, 2):
        cos, sin = turn_sincos((row_id * k).astype(f32) * (1.0 / PADDED))
        for half in range(2):
            rows_t[2 * k - 2, :, pl.ds(128 * half, 128)] = cos
            rows_t[2 * k - 1, :, pl.ds(128 * half, 128)] = sin
    kind = lax.broadcasted_iota(jnp.int32, (8, SHARE), 0)
    col_id = lax.broadcasted_iota(jnp.int32, (8, SHARE), 1) + layer * SHARE
    cos, sin = turn_sincos((col_id * ((kind + 1) // 2)).astype(f32) * (1.0 / PADDED))
    table = jnp.where((kind == 2) | (kind == 4), sin, cos)
    cols_t[...] = jnp.where(kind < 5, table, 0.0)
    acc[...] = jnp.zeros_like(acc)
    loads[2].wait()

    @pl.loop(0, CHUNKS)
    def _(i):
        k = i // 2 + HALF * (1 - i % 2)
        across(1, k).wait_recv()
        upward(k).wait_recv()
        line = facts[pl.ds(8 + k, 1), :]
        piston = jnp.concatenate([line, line], axis=1)
        sums = [jnp.zeros((8, CHUNK), f32) for _ in range(10)]
        cols = pl.ds(pl.multiple_of(k * CHUNK, CHUNK), CHUNK)
        for block in range(8):
            rows = pl.ds(16 * block, 16)
            turns = (
                own[k, rows, :]
                + from_link(x_in[1, k, rows, :])
                + from_link(z_in[k, rows, :])
                + piston
            )
            cos, sin = turn_sincos(turns)
            size = amp[rows, cols].astype(f32)
            real, imag = size * cos, size * sin
            field_re[k, rows, :] = real
            field_im[k, rows, :] = imag
            for base, part in ((0, real), (5, imag)):
                sums[base] = sums[base] + (part[:8] + part[8:])
                for j in range(4):
                    wide = part * rows_t[j, rows, :]
                    sums[base + 1 + j] = sums[base + 1 + j] + (wide[:8] + wide[8:])
        for j in range(10):
            line = jnp.sum(sums[j], axis=0, keepdims=True)
            spread = line * cols_t[:, cols]
            acc[j] = acc[j] + (spread[:, :128] + spread[:, 128:])

    spot = lax.broadcasted_iota(jnp.int32, (8, 128), 1)
    packed = jnp.zeros((8, 128), f32)
    for j in range(10):
        packed = jnp.where(spot == j, jnp.sum(acc[j], axis=1, keepdims=True), packed)
    line_id = lax.broadcasted_iota(jnp.int32, (8, 128), 0)
    total = jnp.where(line_id == 0, packed, 0.0)
    for k in range(1, 5):
        total = total + jnp.where(line_id == k, pltpu.roll(packed, 128 - 16 * k, 1), 0.0)
    total = jnp.sum(total, axis=0, keepdims=True)
    sent = []
    for stage, (size, peer, order) in enumerate(stages):
        message[stage, pl.ds(0, 1), :] = total
        copies = [
            pltpu.make_async_remote_copy(
                src_ref=message.at[stage, pl.ds(0, 1), :],
                dst_ref=arrived.at[stage, pl.ds(d, 1), :],
                send_sem=sum_sem.at[0, stage, d], recv_sem=sum_sem.at[1, stage, d],
                device_id=peer(d), device_id_type=MESH,
            )
            for d in order
        ]
        for copy in copies:
            copy.start()
        for copy in copies:
            copy.wait_recv()
        arrived[stage, pl.ds(0, 1), :] = total
        total = jnp.sum(arrived[stage], axis=0, keepdims=True)
        sent += copies
    total = pltpu.roll(jnp.broadcast_to(total, (8, 128)), 0, 1, stride=16, stride_axis=0)

    row_kind = spot % 5
    col_kind = lax.broadcasted_iota(jnp.int32, (8, 128), 0)
    row_freq = (row_kind + 1) // 2
    col_freq = (col_kind + 1) // 2
    inside = (row_freq * row_freq + col_freq * col_freq <= DOT_RADIUS**2) & (spot < 10)
    factor = (
        jnp.where(inside, 1.0 / (PADDED * PADDED), 0.0)
        * jnp.where(row_kind > 0, 2.0, 1.0)
        * jnp.where(col_kind > 0, 2.0, 1.0)
    )
    turned = jnp.where(spot < 5, -pltpu.roll(total, 123, 1), pltpu.roll(total, 5, 1))
    mix = factor * ((math.cos(phase_step) - 1.0) * total + math.sin(phase_step) * turned)
    for k in range(CHUNKS):
        cols = pl.ds(CHUNK * k, CHUNK)
        lines = [
            jnp.sum(mix[:, j : j + 1] * cols_t[:, cols], axis=0, keepdims=True) for j in range(10)
        ]
        for block in range(8):
            rows = pl.ds(16 * block, 16)
            real = field_re[k, rows, :] + lines[0]
            imag = field_im[k, rows, :] + lines[5]
            for j in range(4):
                table = rows_t[j, rows, :]
                real = real + table * lines[1 + j]
                imag = imag + table * lines[6 + j]
            out[rows, cols] = real * real + imag * imag

    for piece in range(8):
        share(piece).wait_send()
    for copy in sent:
        copy.wait_send()
    for k in range(CHUNKS):
        upward(k).wait_send()
        across(1, k).wait_send()
    for k in range(HALF):
        upward_first(k).wait_send()
        across(0, k + HALF).wait_send()


def body(screens, chosen, row_shift, column_shift, fractions, pistons, segment_map, amplitude):
    hbm = pl.BlockSpec(memory_space=pltpu.HBM)
    vmem = pl.BlockSpec(memory_space=pltpu.VMEM)
    dma = pltpu.SemaphoreType.DMA
    placed, facts = pl.pallas_call(
        place_kernel,
        out_shape=(
            jax.ShapeDtypeStruct((4, 2, ROWS, WIDE), bf16),
            jax.ShapeDtypeStruct((32768, 128), f32),
        ),
        in_specs=[hbm] * 7,
        out_specs=(hbm, hbm),
        scratch_shapes=[
            pltpu.VMEM((16, 128), f32),
            pltpu.SMEM((2,), jnp.int32),
            pltpu.SMEM((2,), jnp.int32),
            pltpu.SMEM((2,), jnp.int32),
            pltpu.SMEM((2, 2), f32),
            pltpu.SMEM(pistons.shape, f32),
            pltpu.SMEM((SEG_GRID, SEG_GRID), jnp.int32),
            pltpu.VMEM((4, 2, ROWS, WIDE), bf16),
            pltpu.VMEM((4, 2, ROWS, WIDE), bf16),
            dma((7,)),
            dma((4, 2)),
            dma((4,)),
        ],
        compiler_params=pltpu.CompilerParams(vmem_limit_bytes=64 * 1024 * 1024),
    )(screens, chosen, row_shift, column_shift, fractions, pistons, segment_map)
    return pl.pallas_call(
        kernel,
        out_shape=jax.ShapeDtypeStruct((ROWS, SHARE), f32),
        in_specs=[hbm, hbm, hbm],
        out_specs=vmem,
        scratch_shapes=[
            pltpu.VMEM((16, 128), f32),
            pltpu.VMEM((ROWS, SHARE), bf16),
            pltpu.VMEM((2, 2, ROWS, WIDE), bf16),
            pltpu.VMEM((2, 2, ROWS, WIDE), bf16),
            pltpu.VMEM((8, 128), f32),
            pltpu.VMEM((1024, CHUNK), bf16),
            pltpu.VMEM((256 * PIECES, 1024), bf16),
            pltpu.VMEM((256 * PIECES, CHUNK), f32),
            pltpu.VMEM((CHUNKS, ROWS, CHUNK), f32),
            pltpu.VMEM((2, CHUNKS, ROWS, CHUNK), LINK),
            pltpu.VMEM((2, CHUNKS, ROWS, CHUNK), LINK),
            pltpu.VMEM((CHUNKS, ROWS, CHUNK), LINK),
            pltpu.VMEM((CHUNKS, ROWS, CHUNK), LINK),
            pltpu.VMEM((HALF, ROWS, CHUNK), LINK),
            pltpu.VMEM((HALF, ROWS, CHUNK), LINK),
            pltpu.VMEM((HALF, ROWS, CHUNK), f32),
            pltpu.VMEM((2, CHUNKS, ROWS, CHUNK), f32),
            pltpu.VMEM((CHUNKS, ROWS, CHUNK), f32),
            pltpu.VMEM((CHUNKS, ROWS, CHUNK), f32),
            pltpu.VMEM((4, ROWS, CHUNK), f32),
            pltpu.VMEM((8, SHARE), f32),
            pltpu.VMEM((10, 8, 128), f32),
            pltpu.VMEM((2, 8, 128), f32),
            pltpu.VMEM((2, 16, 128), f32),
            dma((4,)),
            dma((8,)),
            dma((8,)),
            dma((2,)),
            dma((2, CHUNKS)),
            dma((2, CHUNKS)),
            dma((CHUNKS,)),
            dma((CHUNKS,)),
            dma((HALF,)),
            dma((HALF,)),
            dma((2, 2, 16)),
        ],
        compiler_params=pltpu.CompilerParams(
            collective_id=0, has_side_effects=True, vmem_limit_bytes=52 * 1024 * 1024
        ),
    )(placed, facts, amplitude)


def solution(mesh):
    return jax.shard_map(
        body,
        mesh=mesh,
        in_specs=(
            P("layer", "tile", None),
            P("layer"),
            P("layer"),
            P("layer"),
            P("layer", None),
            P(),
            P(),
            P("tile", None),
        ),
        out_specs=P("tile", "layer"),
        check_vma=False,
    )
```

```python
import functools
import math

import jax
import jax.numpy as jnp
from jax import lax
from jax.experimental import pallas as pl
from jax.experimental.pallas import tpu as pltpu
from jax.sharding import PartitionSpec as P

PUPIL = 8192
PADDED = 16384
SEG_GRID = 32
DOT_RADIUS = 2
ROWS = 128
SHARE = 2048
CHUNK = 256
CHUNKS = SHARE // CHUNK
WIDE = SHARE + 128
PIECES = 2
HALF = CHUNKS // 2
LINK = jnp.bfloat16
SPAN = 500.0
phase_step = math.pi / 2
f32 = jnp.float32
bf16 = jnp.bfloat16
MESH = pl.DeviceIdType.MESH


def nearest(x):
    return jnp.floor(x + 0.5)


def turn_sincos(u):
    r = u - nearest(u)
    q = nearest(4.0 * r)
    x = (r - 0.25 * q) * (2.0 * math.pi)
    z = x * x
    s = x * (1.0 + z * (-1.0 / 6 + z * (1.0 / 120 + z * (-1.0 / 5040 + z * (1.0 / 362880)))))
    c = 1.0 + z * (-0.5 + z * (1.0 / 24 + z * (-1.0 / 720 + z * (1.0 / 40320))))
    odd = jnp.abs(q) == 1.0
    cos = jnp.where(odd, s, c)
    sin = jnp.where(odd, c, s)
    cos = jnp.where((q == 1.0) | (jnp.abs(q) == 2.0), -cos, cos)
    sin = jnp.where((q == -1.0) | (jnp.abs(q) == 2.0), -sin, sin)
    return cos, sin


def to_link(u):
    r = u - nearest(u)
    v = jnp.exp2(jnp.abs(r) * SPAN - 0.25 * SPAN)
    return jnp.where(r < 0.0, -v, v).astype(LINK)


def from_link(v):
    v = v.astype(f32)
    r = jnp.log(jnp.abs(v)) * (1.0 / (math.log(2.0) * SPAN)) + 0.25
    return jnp.where(v < 0.0, -r, r)


def place_kernel(
    screens, chosen_hbm, row_shift_hbm, column_shift_hbm, fractions_hbm, pistons_hbm, map_hbm,
    aligned, facts_hbm,
    facts, chosen, column_shift, row_shift, fractions, pistons, segment_map,
    raw, ready, small_sem, load_sem, store_sem,
):
    small = [
        pltpu.make_async_copy(source, target, small_sem.at[i])
        for i, (source, target) in enumerate(
            (
                (chosen_hbm, chosen),
                (column_shift_hbm, column_shift),
                (row_shift_hbm, row_shift),
                (fractions_hbm, fractions),
                (pistons_hbm, pistons),
                (map_hbm, segment_map),
            )
        )
    ]
    for copy in small:
        copy.start()
    layer = lax.axis_index("layer")
    tile = lax.axis_index("tile")
    sibling = (layer // 2) * 2 + 1 - layer % 2
    order = ((sibling + 2) % 4, (layer + 2) % 4, sibling, layer)

    def load(area, e):
        start = (column_shift[e] // 128 + 16 * area) * 128
        return pltpu.make_async_copy(
            screens.at[chosen[e], :, pl.ds(pl.multiple_of(start, 128), WIDE)],
            raw.at[area, e],
            load_sem.at[area, e],
        )

    def store(area):
        return pltpu.make_async_copy(ready.at[area], aligned.at[area], store_sem.at[area])

    for copy in small[:2]:
        copy.wait()
    for area in order:
        for e in range(2):
            load(area, e).start()
    for copy in small[2:]:
        copy.wait()
    for e in range(2):
        facts[pl.ds(4 * e, 1), :] = jnp.full((1, 128), row_shift[e], jnp.int32).astype(f32)
        facts[pl.ds(4 * e + 1, 1), :] = jnp.full((1, 128), fractions[e, 0], f32)
        facts[pl.ds(4 * e + 2, 1), :] = jnp.full((1, 128), fractions[e, 1], f32)
        facts[pl.ds(4 * e + 3, 1), :] = jnp.zeros((1, 128), f32)
    for k in range(CHUNKS):
        piston = pistons[segment_map[tile // 2, layer * CHUNKS + k]]
        facts[pl.ds(8 + k, 1), :] = jnp.full((1, 128), piston * (0.5 / math.pi), f32)
    keep_facts = pltpu.make_async_copy(facts, facts_hbm.at[pl.ds(0, 16), :], small_sem.at[6])
    keep_facts.start()
    lane = lax.broadcasted_iota(jnp.int32, (ROWS, 128), 1)
    for area in order:
        for e in range(2):
            load(area, e).wait()
            part = column_shift[e] % 128
            keep = lane < 128 - part

            def rolled(j):
                block = raw[area, e, :, pl.ds(128 * j, 128)]
                return pltpu.roll(block, (128 - part) % 128, 1)

            previous = rolled(0)
            for j in range(16):
                following = rolled(j + 1)
                ready[area, e, :, pl.ds(128 * j, 128)] = jnp.where(keep, previous, following)
                previous = following
            ready[area, e, :, pl.ds(SHARE, 128)] = previous
        store(area).start()
    for area in order:
        store(area).wait()
    keep_facts.wait()


def kernel(
    placed, facts_hbm, amplitude, out,
    facts, amp, aligned, shared, sib_prm, taps, weights, product, own,
    x_out, x_in, z_out, z_in, p_out, p_in, held, lows,
    field_re, field_im, rows_t, cols_t, acc, message, arrived,
    load_sem, share_send, share_recv, prm_sem, x_send, x_recv, z_send, z_recv,
    p_send, p_recv, sum_sem,
):
    layer = lax.axis_index("layer")
    tile = lax.axis_index("tile")
    pair, core = layer // 2, layer % 2
    sibling = pair * 2 + 1 - core
    partner = (1 - pair) * 2 + core
    crossed = (1 - pair) * 2 + 1 - core
    before = (tile + 63) % 64
    after = (tile + 1) % 64

    flip = (tile % 32 == 0).astype(jnp.int32)
    target = jnp.where(tile % 32 == 0, partner, layer)
    origin = jnp.where(tile % 32 == 31, partner, layer)
    x = (tile // 32) * 2 + pair
    y = (tile // 8) % 4
    z = tile % 8

    def at(x, y, z, core):
        return (x % 2) * 2 + core, (x // 2) * 32 + y * 8 + z

    def z_peer(d):
        return at(x, y, (z + d) % 8, core)

    def y_peer(d):
        place = (y * 2 + core + d) % 8
        return at(x, place // 2, z, place % 2)

    def x_peer(d):
        return at((x + d) % 4, y, z, core)

    def near_peer(d):
        place = (z * 2 + core + d) % 16
        return at(x, y, place // 2, place % 2)

    def far_peer(d):
        place = (y * 4 + x + d) % 16
        return at(place % 4, place // 4, z, core)

    def ring(step, size):
        return min(step, size - step)

    def near_far(d):
        return -ring(d // 2, 8)

    def far_far(d):
        return -ring(d % 4, 4) - ring(d // 4, 4)

    stages = (
        (16, near_peer, sorted(range(1, 16), key=near_far)),
        (16, far_peer, sorted(range(1, 16), key=far_far)),
    )

    loads = [
        pltpu.make_async_copy(placed.at[area], aligned.at[slot], load_sem.at[slot])
        for slot, area in enumerate((partner, layer))
    ]
    loads.append(
        pltpu.make_async_copy(
            amplitude.at[:, pl.ds(pl.multiple_of(layer * SHARE, SHARE), SHARE)],
            amp,
            load_sem.at[2],
        )
    )
    loads.append(
        pltpu.make_async_copy(facts_hbm.at[pl.ds(0, 16), :], facts, load_sem.at[3])
    )
    for load in loads:
        load.start()

    barrier = pltpu.get_barrier_semaphore()
    greeted = [(sibling, tile), (target, before), (origin, after)]
    greeted += [peer(d) for _, peer, order in stages for d in order]
    for device in greeted:
        pl.semaphore_signal(barrier, inc=1, device_id=device, device_id_type=MESH)

    pl.semaphore_wait(barrier, len(greeted))
    send_prm = pltpu.make_async_remote_copy(
        src_ref=facts.at[pl.ds(0, 8), :], dst_ref=sib_prm, send_sem=prm_sem.at[0], recv_sem=prm_sem.at[1],
        device_id=(sibling, tile), device_id_type=MESH,
    )
    loads[3].wait()
    send_prm.start()
    first, second = (0, 384), (1024, 384)
    rest_first, rest_second = (384, 640), (1408, WIDE - 1408)
    pieces = [(0, second), (0, first), (1, first), (1, second)]
    pieces += [(0, rest_second), (0, rest_first), (1, rest_first), (1, rest_second)]

    def share(piece):
        slot, (start, width) = pieces[piece]
        area = sibling if slot else crossed
        cols = pl.ds(start, width)
        return pltpu.make_async_remote_copy(
            src_ref=placed.at[area, :, :, cols], dst_ref=shared.at[slot, :, :, cols],
            send_sem=share_send.at[piece], recv_sem=share_recv.at[piece],
            device_id=(sibling, tile), device_id_type=MESH,
        )

    for piece in range(8):
        share(piece).start()

    gap = (
        lax.broadcasted_iota(jnp.int32, (256, 128), 1)
        - lax.broadcasted_iota(jnp.int32, (256, 128), 0)
        + 128
    ).astype(f32)
    for source in range(2):
        table = facts if source == 0 else sib_prm
        if source == 1:
            send_prm.wait()
        for e in range(2):
            shift = table[pl.ds(4 * e, 1), :]
            frac_row = table[pl.ds(4 * e + 1, 1), :]
            frac_col = table[pl.ds(4 * e + 2, 1), :]
            down = jnp.where(gap == shift, 1.0 - frac_row, 0.0) + jnp.where(
                gap == shift + 1.0, frac_row, 0.0
            )
            for tap in range(2):
                left = down * ((frac_col if tap else 1.0 - frac_col) * (0.5 / math.pi))
                place = (source * 2 + e) * 256 + tap * 128
                for piece in range(PIECES):
                    part = left.astype(bf16)
                    weights[pl.ds(256 * piece, 256), pl.ds(place, 128)] = part
                    left = left - part.astype(f32)

    def fill(slot, k):
        for source in range(2):
            for e in range(2):
                cols = pl.ds(pl.multiple_of(k * CHUNK, CHUNK), CHUNK + 128)
                block = aligned[slot, e, :, cols] if source == 0 else shared[slot, e, :, cols]
                place = (source * 2 + e) * 256
                taps[pl.ds(place, 128), :] = block[:, :CHUNK]
                moved = pltpu.roll(block, CHUNK + 127, 1)
                taps[pl.ds(place + 128, 128), :] = moved[:, :CHUNK]
        product[...] = jnp.dot(weights[...], taps[...], preferred_element_type=f32)

    def summed(first_row, rows):
        total = product[pl.ds(first_row, rows), :]
        for piece in range(1, PIECES):
            total = total + product[pl.ds(256 * piece + first_row, rows), :]
        return total

    def across(half, k):
        return pltpu.make_async_remote_copy(
            src_ref=x_out.at[half, k], dst_ref=x_in.at[half, k],
            send_sem=x_send.at[half, k], recv_sem=x_recv.at[half, k],
            device_id=(partner, tile), device_id_type=MESH,
        )

    def upward(k):
        return pltpu.make_async_remote_copy(
            src_ref=z_out.at[k], dst_ref=z_in.at[k],
            send_sem=z_send.at[k], recv_sem=z_recv.at[k],
            device_id=(target, before), device_id_type=MESH,
        )

    def upward_first(k):
        return pltpu.make_async_remote_copy(
            src_ref=p_out.at[k], dst_ref=p_in.at[k],
            send_sem=p_send.at[k], recv_sem=p_recv.at[k],
            device_id=(target, before), device_id_type=MESH,
        )

    quarters = [pl.ds(32 * block, 32) for block in range(4)]

    def relay(i):
        upward_first(i).wait_recv()
        for rows in quarters:
            x_out[1, i, rows, :] = to_link(held[i, rows, :] + from_link(p_in[i, rows, :]))
        across(1, i).start()
        k = i + HALF
        across(0, k).wait_recv()
        for rows in quarters:
            z_out[k, rows, :] = to_link(
                lows[1 - flip, k, rows, :] + from_link(x_in[0, k, rows, :])
            )
        upward(k).start()

    loads[0].wait()
    loads[1].wait()

    @pl.loop(0, HALF)
    def _(i):
        k = i + HALF
        def awaited(piece):
            @pl.when(i == 0)
            def _():
                share(piece).wait_recv()

            @pl.when(i == 1)
            def _():
                share(piece + 4).wait_recv()

        def sums(slot, k, target, index, convert):
            fill(slot, k)
            for block, rows in enumerate(quarters):
                target[(*index, rows, slice(None))] = convert(summed(128 + 32 * block, 32))
                lows[slot, k, rows, :] = summed(32 * block, 32)

        awaited(0)
        sums(0, k, x_out, (1, k), to_link)
        across(1, k).start()
        awaited(1)
        sums(0, i, held, (i,), lambda v: v)
        awaited(2)
        sums(1, i, own, (i,), lambda v: v)
        for rows in quarters:
            p_out[i, rows, :] = to_link(lows[flip, i, rows, :])
        upward_first(i).start()
        for rows in quarters:
            z_out[i, rows, :] = to_link(lows[1 - flip, i, rows, :])
        upward(i).start()
        awaited(3)
        sums(1, k, own, (k,), lambda v: v)
        for rows in quarters:
            x_out[0, k, rows, :] = to_link(lows[flip, k, rows, :])
        across(0, k).start()

        @pl.when(i >= 1)
        def _():
            relay(i - 1)

    row_id = lax.broadcasted_iota(jnp.int32, (ROWS, 128), 0) + tile * ROWS
    for k in (1, 2):
        cos, sin = turn_sincos((row_id * k).astype(f32) * (1.0 / PADDED))
        for half in range(2):
            rows_t[2 * k - 2, :, pl.ds(128 * half, 128)] = cos
            rows_t[2 * k - 1, :, pl.ds(128 * half, 128)] = sin
    kind = lax.broadcasted_iota(jnp.int32, (8, SHARE), 0)
    col_id = lax.broadcasted_iota(jnp.int32, (8, SHARE), 1) + layer * SHARE
    cos, sin = turn_sincos((col_id * ((kind + 1) // 2)).astype(f32) * (1.0 / PADDED))
    table = jnp.where((kind == 2) | (kind == 4), sin, cos)
    cols_t[...] = jnp.where(kind < 5, table, 0.0)
    acc[...] = jnp.zeros_like(acc)
    loads[2].wait()

    def finish(i):
        k = i // 2 + HALF * (1 - i % 2)
        across(1, k).wait_recv()
        upward(k).wait_recv()
        line = facts[pl.ds(8 + k, 1), :]
        piston = jnp.concatenate([line, line], axis=1)
        sums = [jnp.zeros((8, CHUNK), f32) for _ in range(10)]
        cols = pl.ds(pl.multiple_of(k * CHUNK, CHUNK), CHUNK)
        for block in range(8):
            rows = pl.ds(16 * block, 16)
            turns = (
                own[k, rows, :]
                + from_link(x_in[1, k, rows, :])
                + from_link(z_in[k, rows, :])
                + piston
            )
            cos, sin = turn_sincos(turns)
            size = amp[rows, cols].astype(f32)
            real, imag = size * cos, size * sin
            field_re[k, rows, :] = real
            field_im[k, rows, :] = imag
            for base, part in ((0, real), (5, imag)):
                sums[base] = sums[base] + (part[:8] + part[8:])
                for j in range(4):
                    wide = part * rows_t[j, rows, :]
                    sums[base + 1 + j] = sums[base + 1 + j] + (wide[:8] + wide[8:])
        for j in range(10):
            line = jnp.sum(sums[j], axis=0, keepdims=True)
            spread = line * cols_t[:, cols]
            acc[j] = acc[j] + (spread[:, :128] + spread[:, 128:])

    pl.loop(0, 3)(finish)
    relay(HALF - 1)
    pl.loop(3, CHUNKS)(finish)

    spot = lax.broadcasted_iota(jnp.int32, (8, 128), 1)
    packed = jnp.zeros((8, 128), f32)
    for j in range(10):
        packed = jnp.where(spot == j, jnp.sum(acc[j], axis=1, keepdims=True), packed)
    line_id = lax.broadcasted_iota(jnp.int32, (8, 128), 0)
    total = jnp.where(line_id == 0, packed, 0.0)
    for k in range(1, 5):
        total = total + jnp.where(line_id == k, pltpu.roll(packed, 128 - 16 * k, 1), 0.0)
    total = jnp.sum(total, axis=0, keepdims=True)
    sent = []
    for stage, (size, peer, order) in enumerate(stages):
        message[stage, pl.ds(0, 1), :] = total
        copies = [
            pltpu.make_async_remote_copy(
                src_ref=message.at[stage, pl.ds(0, 1), :],
                dst_ref=arrived.at[stage, pl.ds(d, 1), :],
                send_sem=sum_sem.at[0, stage, d], recv_sem=sum_sem.at[1, stage, d],
                device_id=peer(d), device_id_type=MESH,
            )
            for d in order
        ]
        for copy in copies:
            copy.start()
        for copy in copies:
            copy.wait_recv()
        arrived[stage, pl.ds(0, 1), :] = total
        total = jnp.sum(arrived[stage], axis=0, keepdims=True)
        sent += copies
    total = pltpu.roll(jnp.broadcast_to(total, (8, 128)), 0, 1, stride=16, stride_axis=0)

    row_kind = spot % 5
    col_kind = lax.broadcasted_iota(jnp.int32, (8, 128), 0)
    row_freq = (row_kind + 1) // 2
    col_freq = (col_kind + 1) // 2
    inside = (row_freq * row_freq + col_freq * col_freq <= DOT_RADIUS**2) & (spot < 10)
    factor = (
        jnp.where(inside, 1.0 / (PADDED * PADDED), 0.0)
        * jnp.where(row_kind > 0, 2.0, 1.0)
        * jnp.where(col_kind > 0, 2.0, 1.0)
    )
    turned = jnp.where(spot < 5, -pltpu.roll(total, 123, 1), pltpu.roll(total, 5, 1))
    mix = factor * ((math.cos(phase_step) - 1.0) * total + math.sin(phase_step) * turned)
    for k in range(CHUNKS):
        cols = pl.ds(CHUNK * k, CHUNK)
        lines = [
            jnp.sum(mix[:, j : j + 1] * cols_t[:, cols], axis=0, keepdims=True) for j in range(10)
        ]
        for block in range(8):
            rows = pl.ds(16 * block, 16)
            real = field_re[k, rows, :] + lines[0]
            imag = field_im[k, rows, :] + lines[5]
            for j in range(4):
                table = rows_t[j, rows, :]
                real = real + table * lines[1 + j]
                imag = imag + table * lines[6 + j]
            out[rows, cols] = real * real + imag * imag

    for piece in range(8):
        share(piece).wait_send()
    for copy in sent:
        copy.wait_send()
    for k in range(CHUNKS):
        upward(k).wait_send()
        across(1, k).wait_send()
    for k in range(HALF):
        upward_first(k).wait_send()
        across(0, k + HALF).wait_send()


def body(screens, chosen, row_shift, column_shift, fractions, pistons, segment_map, amplitude):
    hbm = pl.BlockSpec(memory_space=pltpu.HBM)
    vmem = pl.BlockSpec(memory_space=pltpu.VMEM)
    dma = pltpu.SemaphoreType.DMA
    placed, facts = pl.pallas_call(
        place_kernel,
        out_shape=(
            jax.ShapeDtypeStruct((4, 2, ROWS, WIDE), bf16),
            jax.ShapeDtypeStruct((32768, 128), f32),
        ),
        in_specs=[hbm] * 7,
        out_specs=(hbm, hbm),
        scratch_shapes=[
            pltpu.VMEM((16, 128), f32),
            pltpu.SMEM((2,), jnp.int32),
            pltpu.SMEM((2,), jnp.int32),
            pltpu.SMEM((2,), jnp.int32),
            pltpu.SMEM((2, 2), f32),
            pltpu.SMEM(pistons.shape, f32),
            pltpu.SMEM((SEG_GRID, SEG_GRID), jnp.int32),
            pltpu.VMEM((4, 2, ROWS, WIDE), bf16),
            pltpu.VMEM((4, 2, ROWS, WIDE), bf16),
            dma((7,)),
            dma((4, 2)),
            dma((4,)),
        ],
        compiler_params=pltpu.CompilerParams(vmem_limit_bytes=64 * 1024 * 1024),
    )(screens, chosen, row_shift, column_shift, fractions, pistons, segment_map)
    return pl.pallas_call(
        kernel,
        out_shape=jax.ShapeDtypeStruct((ROWS, SHARE), f32),
        in_specs=[hbm, hbm, hbm],
        out_specs=vmem,
        scratch_shapes=[
            pltpu.VMEM((16, 128), f32),
            pltpu.VMEM((ROWS, SHARE), bf16),
            pltpu.VMEM((2, 2, ROWS, WIDE), bf16),
            pltpu.VMEM((2, 2, ROWS, WIDE), bf16),
            pltpu.VMEM((8, 128), f32),
            pltpu.VMEM((1024, CHUNK), bf16),
            pltpu.VMEM((256 * PIECES, 1024), bf16),
            pltpu.VMEM((256 * PIECES, CHUNK), f32),
            pltpu.VMEM((CHUNKS, ROWS, CHUNK), f32),
            pltpu.VMEM((2, CHUNKS, ROWS, CHUNK), LINK),
            pltpu.VMEM((2, CHUNKS, ROWS, CHUNK), LINK),
            pltpu.VMEM((CHUNKS, ROWS, CHUNK), LINK),
            pltpu.VMEM((CHUNKS, ROWS, CHUNK), LINK),
            pltpu.VMEM((HALF, ROWS, CHUNK), LINK),
            pltpu.VMEM((HALF, ROWS, CHUNK), LINK),
            pltpu.VMEM((HALF, ROWS, CHUNK), f32),
            pltpu.VMEM((2, CHUNKS, ROWS, CHUNK), f32),
            pltpu.VMEM((CHUNKS, ROWS, CHUNK), f32),
            pltpu.VMEM((CHUNKS, ROWS, CHUNK), f32),
            pltpu.VMEM((4, ROWS, CHUNK), f32),
            pltpu.VMEM((8, SHARE), f32),
            pltpu.VMEM((10, 8, 128), f32),
            pltpu.VMEM((2, 8, 128), f32),
            pltpu.VMEM((2, 16, 128), f32),
            dma((4,)),
            dma((8,)),
            dma((8,)),
            dma((2,)),
            dma((2, CHUNKS)),
            dma((2, CHUNKS)),
            dma((CHUNKS,)),
            dma((CHUNKS,)),
            dma((HALF,)),
            dma((HALF,)),
            dma((2, 2, 16)),
        ],
        compiler_params=pltpu.CompilerParams(
            collective_id=0, has_side_effects=True, vmem_limit_bytes=52 * 1024 * 1024
        ),
    )(placed, facts, amplitude)


def solution(mesh):
    return jax.shard_map(
        body,
        mesh=mesh,
        in_specs=(
            P("layer", "tile", None),
            P("layer"),
            P("layer"),
            P("layer"),
            P("layer", None),
            P(),
            P(),
            P("tile", None),
        ),
        out_specs=P("tile", "layer"),
        check_vma=False,
    )
```
